128 devices in a mesh: inst: 8 (over x_hi, y), tp: 16 (over z, x_lo, core).
Axes of the slice: x: 4 (x_hi: 2, x_lo: 2; x = x_hi * 2 + x_lo), y: 4, z: 4, core: 2. Of those that a mesh axis runs over, the one named last changes fastest.
Arguments:
- cache_pool: bfloat16 [1536, 2, 8, 128, 128], P(('inst', 'tp')), may hold values from -20 to 20
- first_query: bfloat16 [32, 16384], P('inst', 'tp'), may hold values from -23 to 23
- second_query: bfloat16 [32, 16384], P('inst', 'tp'), may hold values from -23 to 23
- first_fresh: bfloat16 [32, 2, 1024], P('inst'), may hold values from -5 to 5
- second_fresh: bfloat16 [32, 2, 1024], P('inst'), may hold values from -5 to 5
- first_tables: int32 [32, 32], P('inst'), may hold values from 0 to 191, as said below
- second_tables: int32 [32, 32], P('inst'), may hold values from 0 to 191, as said below
- first_lengths: int32 [32], P('inst'), may hold values from 1 to 4094
- second_lengths: int32 [32], P('inst'), may hold values from 2 to 4095, as said below
- page_moves: int32 [128, 8, 2, 2], P(('inst', 'tp')), may hold values from -1 to 10, as said below
Outputs:
- first_output: bfloat16 [32, 16384], P('inst', 'tp')
- second_output: bfloat16 [32, 16384], P('inst', 'tp')
- cache_after: bfloat16 [1536, 2, 8, 128, 128], P(('inst', 'tp'))
The draws below stay inside these ranges and needn't reach their ends.
Inputs may be any that keep to these rules, and one draw needn't show every extreme that they name: `first_tables`: row s lists the 32 slots reserved for session s in its instance, as t * 12 + l for local slot l of the instance's device with tp index t; the entries of one instance all differ. `second_tables`: rows of sessions that stay equal their first_tables rows; a session that arrived takes the slot of a session that left, and its row names slots that page_moves fills and that no row of first_tables names, each on the device with the same tp index as the page's source slot. `second_lengths`: one more than the first length of the same session: the one that stayed, or for an arrived session the one it came from. `page_moves`: instance i hands exactly one session to each instance (i + r) mod 8 for r = 1 to 2, with all its pages up to its first length; entry [d, b, c] is (source local slot on device d, target local slot on the device of instance b with d's tp index), unused entries are (-1, -1), rows of all other instances are unused; no slot is written twice, and no written slot is a source.
All inputs are finite; a program needn't handle non-finite values.
Results may differ from the reference program's by a relative error of at most 0.0029.
Values may be sent and summed in bfloat16 or wider, within the bound.
A program may use at most 128 MiB of HBM per device.

```python
import jax
import jax.numpy as jnp
from jax import lax

HEADS = 128
KVH = 8
HD = 128
PAGE = 128
SESS = 4
MIG = 2
MAXP = 32
GROUP = 16
CAP = 2
PAGES_DEV = 12
TOT_SESS = 32
NPOOL = 1536
N_INST = 8
N_TP = 16


def place_top(order, region):
    spot = jnp.argmax(order == PAGES_DEV - 1).astype(jnp.int32)
    order = order.at[spot].set(order[0]).at[0].set(PAGES_DEV - 1)
    spot = jnp.argmax(order == PAGES_DEV - 2).astype(jnp.int32)
    return order.at[spot].set(order[region]).at[region].set(PAGES_DEV - 2)


def scenario(key):
    key = jax.random.fold_in(key, 101)
    perm_key, leave_key, length_key, pick_key = jax.random.split(key, 4)
    region = SESS * MAXP // N_TP
    kept = (N_TP + MAXP - 1) // MAXP
    perms = jax.vmap(lambda single: jax.random.permutation(single, PAGES_DEV))(jax.random.split(perm_key, N_INST * N_TP)).astype(jnp.int32)
    perms = jax.vmap(lambda order: place_top(order, region))(perms)
    perms = perms.reshape(N_INST, N_TP, PAGES_DEV).astype(jnp.int32)
    orders = jax.vmap(lambda single: jax.random.permutation(single, SESS - kept))(jax.random.split(leave_key, N_INST)).astype(jnp.int32) + kept
    leaving = orders[:, :MIG]
    first_len = jax.random.randint(length_key, (N_INST, SESS), 1, MAXP * PAGE - 1).astype(jnp.int32)
    pick_inst = jax.random.randint(jax.random.fold_in(pick_key, 1), (), 0, N_INST)
    pick_rank = jax.random.randint(jax.random.fold_in(pick_key, 2), (), 0, MIG)
    first_len = first_len.at[pick_inst, leaving[pick_inst, pick_rank]].set(MAXP * PAGE - 2)
    inst_ids = jnp.arange(N_INST, dtype=jnp.int32)
    ranks = jnp.arange(MIG, dtype=jnp.int32)
    page_ids = jnp.arange(MAXP, dtype=jnp.int32)
    flat_page = jnp.arange(SESS, dtype=jnp.int32)[:, None] * MAXP + page_ids[None, :]
    device_of = flat_page % N_TP
    first_tab = device_of[None] * PAGES_DEV + perms[:, device_of, flat_page // N_TP]
    from_inst = (inst_ids[:, None] - ranks[None, :] - 1) % N_INST
    from_sess = leaving[from_inst, ranks[None, :]]
    arrive_flat = from_sess[:, :, None] * MAXP + page_ids[None, None, :]
    arrive_dev = arrive_flat % N_TP
    arrive_local = region + ranks[None, :, None] * CAP + page_ids[None, None, :] // N_TP
    arrive_local = jnp.broadcast_to(arrive_local, arrive_dev.shape)
    arrive_tab = arrive_dev * PAGES_DEV + perms[jnp.broadcast_to(inst_ids[:, None, None], arrive_dev.shape), arrive_dev, arrive_local]
    second_tab = first_tab.at[inst_ids[:, None], leaving].set(arrive_tab)
    second_len = (first_len + 1).at[inst_ids[:, None], leaving].set(first_len[from_inst, from_sess] + 1)
    to_inst = (inst_ids[:, None] + ranks[None, :] + 1) % N_INST
    send_flat = leaving[:, :, None] * MAXP + page_ids[None, None, :]
    send_dev = send_flat % N_TP
    full_shape = send_dev.shape
    inst_grid = jnp.broadcast_to(inst_ids[:, None, None], full_shape)
    to_grid = jnp.broadcast_to(to_inst[:, :, None], full_shape)
    slot_rank = jnp.broadcast_to(page_ids[None, None, :] // N_TP, full_shape)
    valid = page_ids[None, None, :] <= (first_len[inst_ids[:, None], leaving] // PAGE)[:, :, None]
    src_local = perms[inst_grid, send_dev, send_flat // N_TP]
    dst_local = perms[to_grid, send_dev, region + jnp.broadcast_to(ranks[None, :, None], full_shape) * CAP + slot_rank]
    pairs = jnp.stack([jnp.where(valid, src_local, -1), jnp.where(valid, dst_local, -1)], axis=-1)
    moves = jnp.full((N_INST, N_TP, N_INST, CAP, 2), -1, jnp.int32)
    moves = moves.at[inst_grid, send_dev, to_grid, slot_rank].set(pairs)
    return (first_tab.reshape(TOT_SESS, MAXP), second_tab.reshape(TOT_SESS, MAXP), first_len.reshape(TOT_SESS), second_len.reshape(TOT_SESS), moves.reshape(N_INST * N_TP, N_INST, CAP, 2))


def step_tokens(key, tag_number):
    key = jax.random.fold_in(key, tag_number)
    fresh_key, noise_key = jax.random.split(key, 2)
    fresh_shape = (TOT_SESS, 2, KVH, HD)
    fresh = jnp.clip(jax.random.normal(fresh_key, fresh_shape, jnp.float32), -5.0, 5.0)
    noise_shape = (TOT_SESS, KVH, GROUP, HD)
    noise = jnp.clip(jax.random.normal(noise_key, noise_shape, jnp.float32), -5.0, 5.0)
    query = noise + 0.35 * fresh[:, 0, :, None, :]
    return (fresh.reshape(TOT_SESS, 2, KVH * HD), query.reshape(TOT_SESS, HEADS * HD))


def draw_cache_pool(key, part):
    key = jax.random.fold_in(key, 3)
    first_key = jax.random.fold_in(key, 0)
    pool_shape = (NPOOL, 2, KVH, PAGE, HD)
    drawn = jnp.clip(jax.random.normal(first_key, pool_shape, jnp.float32), -5.0, 5.0)
    return drawn.astype(jnp.bfloat16)


def draw_first_query(key, part):
    tokens = step_tokens(key, 21)
    return tokens[1].astype(jnp.bfloat16)


def draw_second_query(key, part):
    tokens = step_tokens(key, 22)
    return tokens[1].astype(jnp.bfloat16)


def draw_first_fresh(key, part):
    tokens = step_tokens(key, 21)
    return tokens[0].astype(jnp.bfloat16)


def draw_second_fresh(key, part):
    tokens = step_tokens(key, 22)
    return tokens[0].astype(jnp.bfloat16)


def draw_first_tables(key, part):
    plan = scenario(key)
    return plan[0]


def draw_second_tables(key, part):
    plan = scenario(key)
    return plan[1]


def draw_first_lengths(key, part):
    plan = scenario(key)
    return plan[2]


def draw_second_lengths(key, part):
    plan = scenario(key)
    return plan[3]


def draw_page_moves(key, part):
    plan = scenario(key)
    return plan[4]


def setup_inputs(seed: int = 0) -> dict:
    seeds = jax.random.split(jax.random.key(seed), 11)
    cache_pool = draw_cache_pool(jax.random.fold_in(seeds[10], 71), 0)
    first_query = draw_first_query(jax.random.fold_in(seeds[10], 71), 0)
    second_query = draw_second_query(jax.random.fold_in(seeds[10], 71), 0)
    first_fresh = draw_first_fresh(jax.random.fold_in(seeds[10], 71), 0)
    second_fresh = draw_second_fresh(jax.random.fold_in(seeds[10], 71), 0)
    first_tables = draw_first_tables(jax.random.fold_in(seeds[10], 71), 0)
    second_tables = draw_second_tables(jax.random.fold_in(seeds[10], 71), 0)
    first_lengths = draw_first_lengths(jax.random.fold_in(seeds[10], 71), 0)
    second_lengths = draw_second_lengths(jax.random.fold_in(seeds[10], 71), 0)
    page_moves = draw_page_moves(jax.random.fold_in(seeds[10], 71), 0)
    return {"cache_pool": cache_pool, "first_query": first_query, "second_query": second_query, "first_fresh": first_fresh, "second_fresh": second_fresh, "first_tables": first_tables, "second_tables": second_tables, "first_lengths": first_lengths, "second_lengths": second_lengths, "page_moves": page_moves}


def attend_one(query_row, view, length):
    queries = query_row.astype(jnp.float32).reshape(KVH, HEADS // KVH, HD)
    keys_all = view[:, 0].astype(jnp.float32)
    scores = jnp.einsum("kgd,pktd->pkgt", queries, keys_all) * (HD ** -0.5)
    position = jnp.arange(MAXP, dtype=jnp.int32)[:, None] * PAGE + jnp.arange(PAGE, dtype=jnp.int32)[None, :]
    visible = (position <= length)[:, None, None, :]
    page_top = jnp.max(jnp.where(visible, scores, -1e30), axis=3)
    weights = jnp.where(visible, jnp.exp(scores - page_top[..., None]), 0.0)
    rounded = lax.optimization_barrier(weights.astype(jnp.bfloat16))
    page_sum = jnp.einsum("pkgt,pktd->pkgd", rounded.astype(jnp.float32), view[:, 1].astype(jnp.float32))
    page_total = jnp.sum(weights, axis=3)
    overall = jnp.max(page_top, axis=0)
    factor = jnp.exp(page_top - overall)
    numer = jnp.sum(factor[..., None] * page_sum, axis=0)
    denom = jnp.sum(factor * page_total, axis=0)
    return (numer / denom[..., None]).reshape(HEADS * HD).astype(jnp.bfloat16)


def reference(cache_pool, first_query, second_query, first_fresh, second_fresh, first_tables, second_tables, first_lengths, second_lengths, page_moves):
    slots_inst = N_TP * PAGES_DEV
    total_slots = cache_pool.shape[0]
    owner_inst = jnp.arange(TOT_SESS, dtype=jnp.int32) // SESS
    first_global = owner_inst[:, None] * slots_inst + first_tables
    second_global = owner_inst[:, None] * slots_inst + second_tables
    first_page = first_lengths // PAGE
    first_offset = first_lengths % PAGE
    second_offset = second_lengths % PAGE
    first_slot = jnp.take_along_axis(first_global, first_page[:, None], 1)[:, 0]
    second_slot = jnp.take_along_axis(second_global, (second_lengths // PAGE)[:, None], 1)[:, 0]
    fresh_one = first_fresh.reshape(TOT_SESS, 2, KVH, HD)
    fresh_two = second_fresh.reshape(TOT_SESS, 2, KVH, HD)

    def first_step(items):
        query_row, rows_now, length, fresh_row, page_now, offset_now = items
        view = cache_pool[rows_now]
        view = view.at[page_now, :, :, offset_now, :].set(fresh_row)
        return attend_one(query_row, view, length)

    first_output = lax.map(first_step, (first_query, first_global, first_lengths, fresh_one, first_page, first_offset))

    device = jnp.arange(N_INST * N_TP, dtype=jnp.int32)
    source = device[:, None, None] * PAGES_DEV + page_moves[..., 0]
    target = (jnp.arange(N_INST, dtype=jnp.int32)[None, :, None] * N_TP + (device % N_TP)[:, None, None]) * PAGES_DEV + page_moves[..., 1]
    target = jnp.where(page_moves[..., 0] >= 0, target, total_slots)
    anchor = jnp.arange(total_slots, dtype=jnp.int32).at[target.reshape(-1)].set(source.reshape(-1), mode="drop")
    sessions = jnp.arange(TOT_SESS, dtype=jnp.int32)
    first_writer = jnp.full((total_slots,), -1, jnp.int32).at[first_slot].set(sessions)
    second_writer = jnp.full((total_slots,), -1, jnp.int32).at[second_slot].set(sessions)
    token_index = jnp.arange(PAGE, dtype=jnp.int32)[None, :]

    def settle(rows_now):
        moved_from = anchor[rows_now]
        data = cache_pool[moved_from]
        writer = first_writer[moved_from]
        chosen = jnp.maximum(writer, 0)
        hit_one = (writer >= 0)[:, None] & (token_index == first_offset[chosen][:, None])
        data = jnp.where(hit_one[:, None, None, :, None], fresh_one[chosen][:, :, :, None, :], data)
        writer = second_writer[rows_now]
        chosen = jnp.maximum(writer, 0)
        hit_two = (writer >= 0)[:, None] & (token_index == second_offset[chosen][:, None])
        return jnp.where(hit_two[:, None, None, :, None], fresh_two[chosen][:, :, :, None, :], data)

    def second_step(items):
        query_row, rows_now, length = items
        return attend_one(query_row, settle(rows_now), length)

    second_output = lax.map(second_step, (second_query, second_global, second_lengths))
    blocks = jnp.arange(total_slots, dtype=jnp.int32).reshape(N_INST * N_TP, PAGES_DEV)
    cache_after = lax.map(settle, blocks).reshape((total_slots,) + cache_pool.shape[1:])
    return first_output, second_output, cache_after
```

```python
import functools

import jax
import jax.numpy as jnp
from jax import lax
from jax.experimental import pallas as pl
from jax.experimental.pallas import tpu as pltpu
from jax.sharding import PartitionSpec as P

HEADS = 128
KVH = 8
HD = 128
PAGE = 128
SLOTS = 12
SESS = 4
N_INST = 8
N_TP = 16
MESH = pl.DeviceIdType.MESH
TILES = 32
CHUNK = 2
NCH = TILES // CHUNK
HALF = NCH // 2


def iota(shape, dim):
    return lax.broadcasted_iota(jnp.int32, shape, dim)


def put_row(tile, row, fresh):
    fresh = jnp.broadcast_to(fresh.astype(tile.dtype), tile.shape)
    return jnp.where(iota(tile.shape, 0) == row, fresh, tile)


def exchange_kernel(
    scal, meta, tabs, mine, fresh1, cache,
    out_ref, recv_ref, rmeta_ref,
    cbuf, pay, rel, pages, metas, xmine, xtab, fr2, qall, psend, prec, osc, xsend, xrecv,
    load_sem, m_ss, m_rs, x_ss, x_rs, q_ss, q_rs, p_ss, p_rs, o_ss, o_rs,
    g_ss, g_rs, f_ss, f_rs, r_rs,
):
    i = lax.axis_index("inst")
    t = lax.axis_index("tp")
    xh = i // 4
    y = i % 4

    def inst(h, row):
        return lax.rem(h + 2, 2) * 4 + lax.rem(row + 4, 4)

    def at(k):
        return (lax.rem(i + k + N_INST, N_INST), t)

    def peer(u):
        return lax.rem(t + u, N_TP)

    def remote(src, dst, ss, rs, dev):
        return pltpu.make_async_remote_copy(src, dst, ss, rs, device_id=dev, device_id_type=MESH)

    loads = [pltpu.make_async_copy(cache.at[l], cbuf.at[l], load_sem.at[l]) for l in range(SLOTS)]
    for load in loads:
        load.start()

    barrier = pltpu.get_barrier_semaphore()
    for u in range(1, N_TP):
        pl.semaphore_signal(barrier, 1, device_id=(i, peer(u)), device_id_type=MESH)
    for k in range(1, N_INST):
        pl.semaphore_signal(barrier, 1, device_id=at(k), device_id_type=MESH)
    pl.semaphore_wait(barrier, N_TP + N_INST - 2)

    def meta_copy(u):
        return remote(meta, metas.at[t], m_ss.at[u], m_rs.at[t], (i, peer(u)))

    for u in range(1, N_TP):
        meta_copy(u).start()
    cross = []
    for r in (1, 2):
        cross.append(remote(mine, xmine.at[r - 1], x_ss.at[r - 1], x_rs.at[r - 1], at(-r)))
        cross.append(remote(tabs.at[1], xtab.at[r - 1], x_ss.at[1 + r], x_rs.at[1 + r], at(-r)))
        cross.append(remote(meta, rmeta_ref.at[r - 1], x_ss.at[3 + r], x_rs.at[3 + r], at(r)))
    for copy in cross:
        copy.start()

    for load in loads:
        load.wait()

    def make_pay(r):
        for c in range(2):
            e = (r - 1) * 2 + c
            slot = scal[20 + e]
            row = scal[24 + e]
            sess = scal[28 + e]

            def one(n, carry, slot=slot, row=row, sess=sess, c=c):
                fresh = fresh1[sess, pl.ds(n, 1), :]
                pay[r - 1, c * 16 + n] = put_row(cbuf[slot, n], row, fresh)
                return carry

            lax.fori_loop(0, 16, one, 0)

    def chunk(k):
        return pl.ds(k * CHUNK, CHUNK)

    to_relay = {1: (inst(xh, y + 1), t), 2: (inst(xh, y - 1), t)}

    def direct(r, k):
        return remote(
            pay.at[r - 1, chunk(k)], recv_ref.at[r - 1, chunk(k)],
            g_ss.at[r - 1, k], g_rs.at[r - 1, k], at(r),
        )

    def first_leg(r, k):
        return remote(
            pay.at[r - 1, chunk(k)], rel.at[chunk(k)], g_ss.at[r - 1, k], r_rs.at[k], to_relay[r]
        )

    forward_to = {1: (inst(xh + 1, y), t), 2: (inst(xh + jnp.where(y == 1, 1, 0), y - 1), t)}

    def second_leg(r, k):
        return remote(
            rel.at[chunk(k)], recv_ref.at[r - 1, chunk(k)], f_ss.at[k], g_rs.at[r - 1, k], forward_to[r]
        )

    def each(low, high, fn):
        def body(k, carry):
            fn(k)
            return carry

        lax.fori_loop(low, high, body, 0)

    even = y % 2 == 0
    odd = y % 2 == 1
    last = y == 3
    make_pay(2)

    @pl.when(even)
    def _():
        each(0, HALF, lambda k: first_leg(2, k).start())

    make_pay(1)

    @pl.when(last)
    def _():
        each(0, NCH, lambda k: first_leg(1, k).start())

    @pl.when(y < 3)
    def _():
        each(0, NCH, lambda k: direct(1, k).start())

    @pl.when(odd)
    def _():
        each(0, HALF, lambda k: direct(2, k).start())

    each(HALF, NCH, lambda k: direct(2, k).start())

    def relay_step(k):
        @pl.when(y == 0)
        def _():
            first_leg(1, k).wait_recv()
            second_leg(1, k).start()

    def relay_half(k):
        relay_step(k)

        @pl.when(odd)
        def _():
            first_leg(2, k).wait_recv()
            second_leg(2, k).start()

    for u in range(1, N_TP):
        remote(meta, metas.at[peer(u)], m_ss.at[u], m_rs.at[peer(u)], (i, peer(u))).wait_recv()
    for copy in cross:
        copy.wait_recv()
    codes = meta[...]
    for u in range(1, N_TP):
        codes = jnp.maximum(codes, metas[peer(u)])
    rows8 = iota((8, 128), 0)
    left = []
    arrives = []
    for r in (1, 2):
        a_code = codes[2 * r - 2 : 2 * r - 1, :]
        e_code = codes[2 * r - 1 : 2 * r, :]
        left.append(jnp.minimum(jnp.max(jnp.where(tabs[0] == a_code, rows8, 0)), SESS - 1))
        arrives.append(jnp.minimum(jnp.max(jnp.where(xtab[r - 1] == e_code, rows8, 0)), SESS - 1))

    lower = iota((16, 128), 0) >= 8
    for s in range(SESS):
        own = mine[s].astype(jnp.float32)
        query = own[:16]
        fresh = own[16:]
        for r in (0, 1):
            other = xmine[r, arrives[r]].astype(jnp.float32)
            hit = jnp.where(left[r] == s, 1, 0)
            query = jnp.where(lower & (hit == 1), other[:16], query)
            fresh = jnp.where(hit == 1, other[16:], fresh)
        qall[t, s] = query.astype(jnp.bfloat16)
        fr2[s] = fresh

    def q_copy(u):
        return remote(qall.at[t], qall.at[t], q_ss.at[u], q_rs.at[t], (i, peer(u)))

    for u in range(1, N_TP):
        q_copy(u).start()

    for s in range(SESS):
        for j in range(2):
            e = s * 2 + j
            slot = scal[e]
            row1 = scal[16 + s] - scal[8 + e] * PAGE

            def one(n, carry, slot=slot, row1=row1, s=s, e=e):
                tile = put_row(cbuf[slot, n], row1, fresh1[s, pl.ds(n, 1), :])
                pages[e, n] = put_row(tile, row1 + 1, fr2[s, pl.ds(n, 1), :])
                return carry

            lax.fori_loop(0, 16, one, 0)

    for u in range(1, N_TP):
        remote(
            qall.at[t], qall.at[peer(u)], q_ss.at[u], q_rs.at[peer(u)], (i, peer(u))
        ).wait_recv()

    lane = iota((32, 128), 1)
    step_two = (iota((32, 128), 0) // 8) % 2
    lane_group = lane // 16

    def p_copy(dst):
        return remote(psend.at[dst], prec.at[t], p_ss.at[dst], p_rs.at[t], (i, dst))

    def head_step(kk, carry):
        k = lax.rem(kk + t // 2 + 1, KVH)
        stat = jnp.zeros((32, 128), jnp.float32)
        for s in range(SESS):
            query = qall[pl.ds(2 * k, 2), s].reshape(32, HD)
            tops, totals, sums = [], [], []
            for j in range(2):
                e = s * 2 + j
                scores = lax.dot_general(
                    query, pages[e, k], (((1,), (1,)), ((), ())), preferred_element_type=jnp.float32
                ) * (HD ** -0.5)
                visible = lane + scal[8 + e] * PAGE <= scal[16 + s] + step_two
                top = jnp.max(jnp.where(visible, scores, -1e30), axis=1, keepdims=True)
                weight = jnp.where(visible, jnp.exp(scores - top), 0.0)
                tops.append(top)
                totals.append(jnp.sum(weight, axis=1, keepdims=True))
                sums.append(
                    jnp.dot(
                        weight.astype(jnp.bfloat16), pages[e, KVH + k],
                        preferred_element_type=jnp.float32,
                    )
                )
            top = jnp.maximum(tops[0], tops[1])
            f0 = jnp.exp(tops[0] - top)
            f1 = jnp.exp(tops[1] - top)
            psend[pl.ds(2 * k, 2), s] = (f0 * sums[0] + f1 * sums[1]).reshape(2, 16, HD)
            stat = jnp.where(lane_group == 2 * s, top, stat)
            stat = jnp.where(lane_group == 2 * s + 1, f0 * totals[0] + f1 * totals[1], stat)
        psend[pl.ds(2 * k, 2), SESS] = stat.reshape(2, 16, HD)
        for d in range(2):
            @pl.when(2 * k + d != t)
            def _():
                p_copy(2 * k + d).start()
        relay_half(kk)
        return carry

    lax.fori_loop(0, KVH, head_step, 0)
    each(HALF, HALF + 4, relay_step)

    for u in range(1, N_TP):
        remote(
            psend.at[t], prec.at[peer(u)], p_ss.at[t], p_rs.at[peer(u)], (i, peer(u))
        ).wait_recv()
    prec[t] = psend[t]

    def top_step(u, best):
        return jnp.maximum(best, prec[u, SESS])

    best = lax.fori_loop(1, N_TP, top_step, prec[0, SESS])

    def sum_step(u, carry):
        acc, tot = carry
        stat = prec[u, SESS]
        factor = jnp.exp(stat - best)
        new_acc = []
        new_tot = []
        for s in range(SESS):
            f = factor[:, 32 * s : 32 * s + 1]
            new_acc.append(acc[s] + f * prec[u, s])
            new_tot.append(tot[s] + f * stat[:, 32 * s + 16 : 32 * s + 17])
        return tuple(new_acc), tuple(new_tot)

    zero = jnp.zeros((16, HD), jnp.float32)
    none = jnp.zeros((16, 1), jnp.float32)
    acc, tot = lax.fori_loop(0, N_TP, sum_step, ((zero,) * SESS, (none,) * SESS))
    for s in range(SESS):
        osc[s] = acc[s] / tot[s]

    for r in (0, 1):
        row = osc[left[r]]
        for s in range(SESS):
            xsend[r, s] = jnp.where(arrives[r] == s, row, 0.0).astype(jnp.bfloat16)
    outs = [remote(xsend.at[r], xrecv.at[r], o_ss.at[r], o_rs.at[r], at(r + 1)) for r in (0, 1)]
    for copy in outs:
        copy.start()
    each(HALF + 4, NCH, relay_step)
    for copy in outs:
        copy.wait_recv()
    for s in range(SESS):
        gone = jnp.where((left[0] == s) | (left[1] == s), 1, 0)
        came = xrecv[0, s].astype(jnp.float32) + xrecv[1, s].astype(jnp.float32)
        out_ref[s] = jnp.where(lower & (gone == 1), came, osc[s]).astype(jnp.bfloat16)

    for u in range(1, N_TP):
        meta_copy(u).wait_send()
        q_copy(u).wait_send()
        p_copy(peer(u)).wait_send()
    for copy in cross + outs:
        copy.wait_send()
    for r in (1, 2):
        each(0, NCH, lambda k, r=r: direct(r, k).wait_send())

    @pl.when(y == 0)
    def _():
        each(0, NCH, lambda k: second_leg(1, k).wait_send())

    @pl.when(odd)
    def _():
        each(0, HALF, lambda k: second_leg(2, k).wait_send())

    for r in (1, 2):
        each(0, NCH, lambda k, r=r: direct(r, k).wait_recv())


def exchange(scal, meta, tabs, mine, fresh1, cache):
    vmem = pl.BlockSpec(memory_space=pltpu.VMEM)
    hbm = pl.BlockSpec(memory_space=pl.ANY)
    dma = pltpu.SemaphoreType.DMA
    bf16, f32, i32 = jnp.bfloat16, jnp.float32, jnp.int32
    return pl.pallas_call(
        exchange_kernel,
        name="exchange",
        out_shape=(
            jax.ShapeDtypeStruct((SESS, 16, HD), bf16),
            jax.ShapeDtypeStruct((2, TILES, PAGE, HD), bf16),
            jax.ShapeDtypeStruct((2, 8, 128), i32),
        ),
        in_specs=[pl.BlockSpec(memory_space=pltpu.SMEM), vmem, vmem, vmem, vmem, hbm],
        out_specs=(vmem, hbm, vmem),
        scratch_shapes=[
            pltpu.VMEM((SLOTS, 16, PAGE, HD), bf16),
            pltpu.VMEM((2, TILES, PAGE, HD), bf16),
            pltpu.VMEM((TILES, PAGE, HD), bf16),
            pltpu.VMEM((2 * SESS, 16, PAGE, HD), bf16),
            pltpu.VMEM((N_TP, 8, 128), i32),
            pltpu.VMEM((2, SESS, 32, HD), bf16),
            pltpu.VMEM((2, 8, 128), i32),
            pltpu.VMEM((SESS, 16, HD), f32),
            pltpu.VMEM((N_TP, SESS, 16, HD), bf16),
            pltpu.VMEM((N_TP, SESS + 1, 16, HD), f32),
            pltpu.VMEM((N_TP, SESS + 1, 16, HD), f32),
            pltpu.VMEM((SESS, 16, HD), f32),
            pltpu.VMEM((2, SESS, 16, HD), bf16),
            pltpu.VMEM((2, SESS, 16, HD), bf16),
            dma((SLOTS,)),
            dma((N_TP,)), dma((N_TP,)),
            dma((6,)), dma((6,)),
            dma((N_TP,)), dma((N_TP,)),
            dma((N_TP,)), dma((N_TP,)),
            dma((2,)), dma((2,)),
            dma((2, NCH)), dma((2, NCH)),
            dma((NCH,)), dma((NCH,)),
            dma((NCH,)),
        ],
        compiler_params=pltpu.CompilerParams(
            collective_id=1, has_side_effects=True, vmem_limit_bytes=32 * 1024 * 1024
        ),
    )(scal, meta, tabs, mine, fresh1, cache)


def assemble_kernel(plan, came, fresh, cache, recv, out, buf, in_sem, out_sem):
    targets = [came[r, 4 + 2 * r + c, 0] for r in range(2) for c in range(2)]
    for n, target in enumerate(targets):
        @pl.when(target >= 0)
        def _():
            pltpu.make_async_copy(
                recv.at[n // 2, pl.ds((n % 2) * 16, 16)], buf.at[target], in_sem.at[target]
            ).start()
    for l in range(SLOTS):
        hit = functools.reduce(jnp.logical_or, [target == l for target in targets])

        @pl.when(jnp.logical_not(hit))
        def _():
            pltpu.make_async_copy(cache.at[l], buf.at[l], in_sem.at[l]).start()
    for l in range(SLOTS):
        pltpu.make_async_copy(cache.at[l], buf.at[l], in_sem.at[l]).wait()
    for step in range(2):
        for s in range(SESS):
            slot = plan[step, s]
            row = plan[2 + step, s]

            @pl.when(slot >= 0)
            def _():
                start = pl.multiple_of((row // 16) * 16, 16)

                def one(n, carry):
                    tile = buf[slot, n, pl.ds(start, 16), :]
                    buf[slot, n, pl.ds(start, 16), :] = put_row(
                        tile, row - start, fresh[step, s, pl.ds(n, 1), :]
                    )
                    return carry

                lax.fori_loop(0, 16, one, 0)
    outs = [pltpu.make_async_copy(buf.at[l], out.at[l], out_sem.at[l]) for l in range(SLOTS)]
    for copy in outs:
        copy.start()
    for copy in outs:
        copy.wait()


def assemble(plan, came, fresh, cache, recv):
    vmem = pl.BlockSpec(memory_space=pltpu.VMEM)
    hbm = pl.BlockSpec(memory_space=pl.ANY)
    smem = pl.BlockSpec(memory_space=pltpu.SMEM)
    return pl.pallas_call(
        assemble_kernel,
        name="assemble",
        out_shape=jax.ShapeDtypeStruct(cache.shape, cache.dtype),
        in_specs=[smem, smem, vmem, hbm, hbm],
        out_specs=hbm,
        scratch_shapes=[
            pltpu.VMEM((SLOTS, 16, PAGE, HD), jnp.bfloat16),
            pltpu.SemaphoreType.DMA((SLOTS,)),
            pltpu.SemaphoreType.DMA((SLOTS,)),
        ],
        compiler_params=pltpu.CompilerParams(vmem_limit_bytes=16 * 1024 * 1024),
    )(plan, came, fresh, cache, recv)


def token_place(tables, lengths, tp_index):
    named = jnp.take_along_axis(tables, (lengths // PAGE)[:, None], 1)[:, 0]
    return jnp.where(named // SLOTS == tp_index, named % SLOTS, -1), lengths % PAGE


def shards(
    cache_pool,
    first_query,
    second_query,
    first_fresh,
    second_fresh,
    first_tables,
    second_tables,
    first_lengths,
    second_lengths,
    page_moves,
):
    t = lax.axis_index("tp")
    i = lax.axis_index("inst")
    cache = cache_pool.reshape(SLOTS, 16, PAGE, HD)

    column = jnp.arange(first_tables.shape[1], dtype=jnp.int32)[None, :]
    here = first_tables // SLOTS == t
    number = jnp.stack(
        [
            jnp.min(jnp.where(here, column, first_tables.shape[1] - 1), axis=1),
            jnp.max(jnp.where(here, column, 0), axis=1),
        ],
        axis=1,
    )
    slot = jnp.sum(
        jnp.where(column[:, None, :] == number[:, :, None], first_tables[:, None, :] % SLOTS, 0), axis=2
    )
    moves = jnp.stack(
        [lax.dynamic_index_in_dim(page_moves[0], (i + r) % N_INST, 0, keepdims=False) for r in (1, 2)]
    )
    source, target = moves[..., 0], moves[..., 1]
    pay_slot = jnp.maximum(source, 0).reshape(4)
    mine_of = pay_slot[:, None, None] == slot[None]
    pay_sess = jnp.sum(
        jnp.where(mine_of, jnp.arange(SESS, dtype=jnp.int32)[None, :, None], 0), axis=(1, 2)
    )
    first_row = first_lengths[:, None] - number * PAGE
    pay_row = jnp.sum(jnp.where(mine_of, first_row[None], 0), axis=(1, 2))
    scal = jnp.concatenate(
        [slot.reshape(8), number.reshape(8), first_lengths, pay_slot, pay_row, pay_sess]
    )
    codes = jnp.stack(
        [
            jnp.max(jnp.where(source >= 0, t * SLOTS + source, -1), axis=1),
            jnp.max(jnp.where(target >= 0, t * SLOTS + target, -1), axis=1),
        ],
        axis=1,
    ).reshape(4)
    meta = jnp.broadcast_to(jnp.concatenate([codes, target.reshape(4)])[:, None], (8, 128))
    tabs = jnp.pad(
        jnp.stack([first_tables, second_tables]), ((0, 0), (0, 4), (0, 96)), constant_values=-2
    )
    mine = jnp.concatenate(
        [
            first_query.reshape(SESS, 8, HD),
            second_query.reshape(SESS, 8, HD),
            second_fresh.reshape(SESS, 16, HD),
        ],
        axis=1,
    )
    fresh = jnp.stack([first_fresh.reshape(SESS, 16, HD), second_fresh.reshape(SESS, 16, HD)])
    fresh = fresh.astype(jnp.float32)
    out, recv, came = exchange(scal, meta, tabs, mine, fresh[0], cache)

    slot_one, row_one = token_place(first_tables, first_lengths, t)
    slot_two, row_two = token_place(second_tables, second_lengths, t)
    plan = jnp.stack([slot_one, slot_two, row_one, row_two])
    cache_after = assemble(plan, came, fresh, cache, recv)
    return (
        out[:, :8].reshape(SESS, 8 * HD),
        out[:, 8:].reshape(SESS, 8 * HD),
        cache_after.reshape(cache_pool.shape),
    )


def solution(mesh):
    placed = (
        P(("inst", "tp"), None, None, None, None),
        P("inst", "tp"),
        P("inst", "tp"),
        P("inst", None, None),
        P("inst", None, None),
        P("inst", None),
        P("inst", None),
        P("inst"),
        P("inst"),
        P(("inst", "tp"), None, None, None),
    )
    return jax.shard_map(
        shards,
        mesh=mesh,
        in_specs=placed,
        out_specs=(P("inst", "tp"), P("inst", "tp"), P(("inst", "tp"), None, None, None, None)),
        check_vma=False,
    )
```

```python
import functools

import jax
import jax.numpy as jnp
from jax import lax
from jax.experimental import pallas as pl
from jax.experimental.pallas import tpu as pltpu
from jax.sharding import PartitionSpec as P

HEADS = 128
KVH = 8
HD = 128
PAGE = 128
SLOTS = 12
SESS = 4
N_INST = 8
N_TP = 16
MESH = pl.DeviceIdType.MESH
TILES = 32
CHUNK = 2
NCH = TILES // CHUNK
HALF = NCH // 2
BIG = 8
NBIG = TILES // BIG


def iota(shape, dim):
    return lax.broadcasted_iota(jnp.int32, shape, dim)


def one_hot(row):
    hot = jnp.where(iota((PAGE, HD), 0) == row, 1.0, 0.0).astype(jnp.bfloat16)
    return hot.reshape(8, 16, HD)


def spread(row):
    return jnp.broadcast_to(row, (16, HD)).astype(jnp.bfloat16)[None]


def heads_apart(flat, into, row):
    for h in range(KVH):
        into[:, row + h, :] = flat[:, h * HD : (h + 1) * HD].astype(into.dtype)


def exchange_kernel(
    ft, n1, moves, first_tab, second_tab, first_query, second_query, first_fresh, second_fresh, cache,
    out_ref, recv_ref, rmeta_ref,
    cbuf, pay, rel, pages, meta, metas, mytab, xtab, mine32, fr1, mine, xmine, fr2, qall, psend, prec,
    osc, xsend, xrecv,
    load_sem, m_ss, m_rs, x_ss, x_rs, q_ss, q_rs, p_ss, p_rs, o_ss, o_rs,
    g_ss, g_rs, f_ss, f_rs, r_rs,
):
    i = lax.axis_index("inst")
    t = lax.axis_index("tp")
    xh = i // 4
    y = i % 4

    def inst(h, row):
        return lax.rem(h + 2, 2) * 4 + lax.rem(row + 4, 4)

    def at(k):
        return (lax.rem(i + k + N_INST, N_INST), t)

    def peer(u):
        return lax.rem(t + u, N_TP)

    def remote(src, dst, ss, rs, dev):
        return pltpu.make_async_remote_copy(src, dst, ss, rs, device_id=dev, device_id_type=MESH)

    loads = [pltpu.make_async_copy(cache.at[l], cbuf.at[l], load_sem.at[l]) for l in range(SLOTS)]
    for load in loads:
        load.start()

    barrier = pltpu.get_barrier_semaphore()
    for u in range(1, N_TP):
        pl.semaphore_signal(barrier, 1, device_id=(i, peer(u)), device_id_type=MESH)
    for k in range(1, N_INST):
        pl.semaphore_signal(barrier, 1, device_id=at(k), device_id_type=MESH)

    low = t * SLOTS
    slots, numbers = [], []
    for s in range(SESS):
        def look(p, found, s=s):
            slot0, slot1, page0, page1 = found
            v = ft[s, p] - low
            hit = (v >= 0) & (v < SLOTS)
            new = hit & (page0 < 0)
            return (
                jnp.where(new, v, slot0), jnp.where(hit, v, slot1),
                jnp.where(new, p, page0), jnp.where(hit, p, page1),
            )

        zero, none = jnp.int32(0), jnp.int32(-1)
        slot0, slot1, page0, page1 = lax.fori_loop(0, 32, look, (zero, zero, none, none), unroll=8)
        slots += [slot0, slot1]
        numbers += [page0, page1]

    rows8 = iota((8, 128), 0)
    sources, targets = {}, {}
    table = jnp.zeros((8, 128), jnp.int32)
    for r in (1, 2):
        b = lax.rem(i + r, N_INST)
        a_code = e_code = jnp.int32(-1)
        for c in range(2):
            a, e = moves[0, b, c, 0], moves[0, b, c, 1]
            sources[r, c] = a
            a_code = jnp.maximum(a_code, jnp.where(a >= 0, low + a, -1))
            e_code = jnp.maximum(e_code, jnp.where(e >= 0, low + e, -1))
            table = jnp.where(rows8 == 4 + 2 * (r - 1) + c, e, table)
        table = jnp.where(rows8 == 2 * r - 2, a_code, table)
        table = jnp.where(rows8 == 2 * r - 1, e_code, table)
    meta[...] = table
    mytab[...] = jnp.full((8, 128), -2, jnp.int32)
    mytab[0:SESS, 0:32] = second_tab[...]
    heads_apart(first_query[...].astype(jnp.float32), mine32, 0)
    heads_apart(second_query[...].astype(jnp.float32), mine32, 8)
    for s in range(SESS):
        token = first_fresh[s].astype(jnp.float32)
        other = second_fresh[s].astype(jnp.float32)
        for h in range(KVH):
            fr1[s, :, h, :] = token[:, h * HD : (h + 1) * HD]
            for kv in range(2):
                mine32[s, 16 + kv * 8 + h, :] = other[kv, h * HD : (h + 1) * HD]
    for s in range(SESS):
        mine[s] = mine32[s].astype(jnp.bfloat16)

    for load in loads:
        load.wait()

    def make_pay(r):
        for c in range(2):
            slot = jnp.maximum(sources[r, c], 0)
            sess = row = jnp.int32(0)
            for e in range(2 * SESS):
                mine_is = slots[e] == slot
                sess = jnp.where(mine_is, e // 2, sess)
                row = jnp.where(mine_is, n1[e // 2] - numbers[e] * PAGE, row)
            hot = one_hot(row)
            keep = 1 - hot

            def one(n, carry, slot=slot, sess=sess, hot=hot, keep=keep, c=c):
                fresh = spread(fr1[sess, n // 8, pl.ds(n % 8, 1), :])
                tile = cbuf[slot, n].reshape(8, 16, HD) * keep + fresh * hot
                pay[r - 1, c * 16 + n] = tile.reshape(PAGE, HD)
                return carry

            lax.fori_loop(0, 16, one, 0, unroll=4)

    make_pay(1)
    make_pay(2)
    pl.semaphore_wait(barrier, N_TP + N_INST - 2)

    def meta_copy(u):
        return remote(meta, metas.at[t], m_ss.at[u], m_rs.at[t], (i, peer(u)))

    for u in range(1, N_TP):
        meta_copy(u).start()
    cross = []
    for r in (1, 2):
        cross.append(remote(mine, xmine.at[r - 1], x_ss.at[r - 1], x_rs.at[r - 1], at(-r)))
        cross.append(remote(mytab, xtab.at[r - 1], x_ss.at[1 + r], x_rs.at[1 + r], at(-r)))
        cross.append(remote(meta, rmeta_ref.at[r - 1], x_ss.at[3 + r], x_rs.at[3 + r], at(r)))
    for copy in cross:
        copy.start()

    def chunk(k):
        return pl.ds(k * CHUNK, CHUNK)

    to_relay = {1: (inst(xh, y + 1), t), 2: (inst(xh, y - 1), t)}

    def direct(r, q):
        tiles = pl.ds(q * BIG, BIG)
        return remote(
            pay.at[r - 1, tiles], recv_ref.at[r - 1, tiles],
            g_ss.at[r - 1, NCH + q], g_rs.at[r - 1, NCH + q], at(r),
        )

    def first_leg(r, k):
        return remote(
            pay.at[r - 1, chunk(k)], rel.at[chunk(k)], g_ss.at[r - 1, k], r_rs.at[k], to_relay[r]
        )

    forward_to = {1: (inst(xh + 1, y), t), 2: (inst(xh + jnp.where(y == 1, 1, 0), y - 1), t)}

    def second_leg(r, k):
        return remote(
            rel.at[chunk(k)], recv_ref.at[r - 1, chunk(k)], f_ss.at[k], g_rs.at[r - 1, k], forward_to[r]
        )

    def each(low, high, fn):
        def body(k, carry):
            fn(k)
            return carry

        lax.fori_loop(low, high, body, 0)

    even = y % 2 == 0
    odd = y % 2 == 1
    last = y == 3
    @pl.when(even)
    def _():
        each(0, HALF, lambda k: first_leg(2, k).start())

    @pl.when(last)
    def _():
        each(0, NCH, lambda k: first_leg(1, k).start())

    @pl.when(y < 3)
    def _():
        each(0, NBIG, lambda q: direct(1, q).start())

    def relay_one(low, high):
        @pl.when(y == 0)
        def _():
            def step(k):
                first_leg(1, k).wait_recv()
                second_leg(1, k).start()

            each(low, high, step)

    def relay_two(low, high):
        @pl.when(odd)
        def _():
            def step(k):
                first_leg(2, k).wait_recv()
                second_leg(2, k).start()

            each(low, high, step)

    for u in range(1, N_TP):
        remote(meta, metas.at[peer(u)], m_ss.at[u], m_rs.at[peer(u)], (i, peer(u))).wait_recv()
    for copy in cross:
        copy.wait_recv()
    codes = meta[...]
    for u in range(1, N_TP):
        codes = jnp.maximum(codes, metas[peer(u)])
    left = []
    arrives = []
    for r in (1, 2):
        a_code = codes[2 * r - 2 : 2 * r - 1, :]
        e_code = codes[2 * r - 1 : 2 * r, :]
        left.append(jnp.minimum(jnp.max(jnp.where(first_tab[...] == a_code[:, :32], rows8[:SESS, :32], 0)), SESS - 1))
        arrives.append(jnp.minimum(jnp.max(jnp.where(xtab[r - 1] == e_code, rows8, 0)), SESS - 1))

    relay_two(0, 2)
    relay_one(0, 2)

    lower = iota((16, 128), 0) >= 8
    for s in range(SESS):
        own = mine[s].astype(jnp.float32)
        query = own[:16]
        fresh = own[16:]
        for r in (0, 1):
            other = xmine[r, arrives[r]].astype(jnp.float32)
            hit = jnp.where(left[r] == s, 1, 0)
            query = jnp.where(lower & (hit == 1), other[:16], query)
            fresh = jnp.where(hit == 1, other[16:], fresh)
        qall[t, s] = query.astype(jnp.bfloat16)
        fr2[s] = fresh

    def q_copy(u):
        return remote(qall.at[t], qall.at[t], q_ss.at[u], q_rs.at[t], (i, peer(u)))

    for u in range(1, N_TP):
        q_copy(u).start()

    for s in range(SESS):
        for j in range(2):
            e = s * 2 + j
            slot = slots[e]
            row1 = n1[s] - numbers[e] * PAGE
            hot1 = one_hot(row1)
            hot2 = one_hot(row1 + 1)
            keep = 1 - hot1 - hot2

            def one(n, carry, slot=slot, hot1=hot1, hot2=hot2, keep=keep, s=s, e=e):
                fresh1 = spread(fr1[s, n // 8, pl.ds(n % 8, 1), :])
                fresh2 = spread(fr2[s, pl.ds(n, 1), :])
                tile = cbuf[slot, n].reshape(8, 16, HD) * keep + fresh1 * hot1 + fresh2 * hot2
                pages[e, n] = tile.reshape(PAGE, HD)
                return carry

            lax.fori_loop(0, 16, one, 0, unroll=4)

    relay_two(2, 4)
    relay_one(2, 3)
    for u in range(1, N_TP):
        remote(
            qall.at[t], qall.at[peer(u)], q_ss.at[u], q_rs.at[peer(u)], (i, peer(u))
        ).wait_recv()

    relay_two(4, HALF)

    @pl.when(odd)
    def _():
        each(0, NBIG, lambda q: direct(2, q).start())

    relay_one(3, 6)

    lane = iota((32, 128), 1)
    step_two = (iota((32, 128), 0) // 8) % 2
    lane_group = lane // 16

    def p_copy(dst):
        return remote(psend.at[dst], prec.at[t], p_ss.at[dst], p_rs.at[t], (i, dst))

    def head_step(kk, carry):
        k = lax.rem(kk + t // 2 + 1, KVH)
        stat = jnp.zeros((32, 128), jnp.float32)
        for s in range(SESS):
            query = qall[pl.ds(2 * k, 2), s].reshape(32, HD)
            keys = pages[pl.ds(2 * s, 2), k].reshape(2 * PAGE, HD)
            both = lax.dot_general(
                query, keys, (((1,), (1,)), ((), ())), preferred_element_type=jnp.float32
            ) * (HD ** -0.5)
            tops, totals, sums = [], [], []
            for j in range(2):
                e = s * 2 + j
                scores = both[:, j * PAGE : (j + 1) * PAGE]
                visible = lane + numbers[e] * PAGE <= n1[s] + step_two
                top = jnp.max(jnp.where(visible, scores, -1e30), axis=1, keepdims=True)
                weight = jnp.where(visible, jnp.exp(scores - top), 0.0)
                tops.append(top)
                totals.append(jnp.sum(weight, axis=1, keepdims=True))
                sums.append(
                    jnp.dot(
                        weight.astype(jnp.bfloat16), pages[e, KVH + k],
                        preferred_element_type=jnp.float32,
                    )
                )
            top = jnp.maximum(tops[0], tops[1])
            f0 = jnp.exp(tops[0] - top)
            f1 = jnp.exp(tops[1] - top)
            psend[pl.ds(2 * k, 2), s] = (f0 * sums[0] + f1 * sums[1]).reshape(2, 16, HD)
            stat = jnp.where(lane_group == 2 * s, top, stat)
            stat = jnp.where(lane_group == 2 * s + 1, f0 * totals[0] + f1 * totals[1], stat)
        psend[pl.ds(2 * k, 2), SESS] = stat.reshape(2, 16, HD)
        for d in range(2):
            @pl.when(2 * k + d != t)
            def _():
                p_copy(2 * k + d).start()
        relay_one(kk + 6, kk + 7)
        return carry

    lax.fori_loop(0, KVH, head_step, 0)
    relay_one(NCH - 2, NCH)

    @pl.when(last)
    def _():
        each(0, NCH, lambda k: first_leg(1, k).wait_send())

    @pl.when(y < 3)
    def _():
        each(0, NBIG, lambda q: direct(1, q).wait_send())

    @pl.when(even)
    def _():
        each(NBIG // 2, NBIG, lambda q: direct(2, q).start())

    for u in range(1, N_TP):
        remote(
            psend.at[t], prec.at[peer(u)], p_ss.at[t], p_rs.at[peer(u)], (i, peer(u))
        ).wait_recv()
    prec[t] = psend[t]
    def top_step(u, best):
        return jnp.maximum(best, prec[u, SESS])

    best = lax.fori_loop(1, N_TP, top_step, prec[0, SESS])

    def sum_step(u, carry):
        acc, tot = carry
        stat = prec[u, SESS]
        factor = jnp.exp(stat - best)
        new_acc = []
        new_tot = []
        for s in range(SESS):
            f = factor[:, 32 * s : 32 * s + 1]
            new_acc.append(acc[s] + f * prec[u, s])
            new_tot.append(tot[s] + f * stat[:, 32 * s + 16 : 32 * s + 17])
        return tuple(new_acc), tuple(new_tot)

    zero = jnp.zeros((16, HD), jnp.float32)
    none = jnp.zeros((16, 1), jnp.float32)
    acc, tot = lax.fori_loop(0, N_TP, sum_step, ((zero,) * SESS, (none,) * SESS))
    for s in range(SESS):
        osc[s] = acc[s] / tot[s]

    for r in (0, 1):
        row = osc[left[r]]
        for s in range(SESS):
            xsend[r, s] = jnp.where(arrives[r] == s, row, 0.0).astype(jnp.bfloat16)
    outs = [remote(xsend.at[r], xrecv.at[r], o_ss.at[r], o_rs.at[r], at(r + 1)) for r in (0, 1)]
    for copy in outs:
        copy.start()
    for copy in outs:
        copy.wait_recv()
    for s in range(SESS):
        gone = jnp.where((left[0] == s) | (left[1] == s), 1, 0)
        came = xrecv[0, s].astype(jnp.float32) + xrecv[1, s].astype(jnp.float32)
        out_ref[s] = jnp.where(lower & (gone == 1), came, osc[s])

    for u in range(1, N_TP):
        meta_copy(u).wait_send()
        q_copy(u).wait_send()
        p_copy(peer(u)).wait_send()
    for copy in cross + outs:
        copy.wait_send()
    @pl.when(y == 0)
    def _():
        each(0, NCH, lambda k: second_leg(1, k).wait_send())

    @pl.when(odd)
    def _():
        each(0, HALF, lambda k: second_leg(2, k).wait_send())
        each(0, NBIG, lambda q: direct(2, q).wait_send())

    @pl.when(even)
    def _():
        each(0, HALF, lambda k: first_leg(2, k).wait_send())
        each(NBIG // 2, NBIG, lambda q: direct(2, q).wait_send())

    @pl.when(y == 0)
    def _():
        each(0, NCH, lambda k: second_leg(1, k).wait_recv())

    @pl.when(y > 0)
    def _():
        each(0, NBIG, lambda q: direct(1, q).wait_recv())

    @pl.when(odd)
    def _():
        each(0, NBIG, lambda q: direct(2, q).wait_recv())

    @pl.when(even)
    def _():
        each(0, HALF, lambda k: second_leg(2, k).wait_recv())
        each(NBIG // 2, NBIG, lambda q: direct(2, q).wait_recv())


def exchange(ft, n1, moves, st, first_query, second_query, first_fresh, second_fresh, cache):
    vmem = pl.BlockSpec(memory_space=pltpu.VMEM)
    smem = pl.BlockSpec(memory_space=pltpu.SMEM)
    hbm = pl.BlockSpec(memory_space=pl.ANY)
    dma = pltpu.SemaphoreType.DMA
    bf16, f32, i32 = jnp.bfloat16, jnp.float32, jnp.int32
    return pl.pallas_call(
        exchange_kernel,
        name="exchange",
        out_shape=(
            jax.ShapeDtypeStruct((SESS, 16, HD), f32),
            jax.ShapeDtypeStruct((2, TILES, PAGE, HD), bf16),
            jax.ShapeDtypeStruct((2, 8, 128), i32),
        ),
        in_specs=[smem, smem, smem] + [vmem] * 6 + [hbm],
        out_specs=(vmem, hbm, vmem),
        scratch_shapes=[
            pltpu.VMEM((SLOTS, 16, PAGE, HD), bf16),
            pltpu.VMEM((2, TILES, PAGE, HD), bf16),
            pltpu.VMEM((TILES, PAGE, HD), bf16),
            pltpu.VMEM((2 * SESS, 16, PAGE, HD), bf16),
            pltpu.VMEM((8, 128), i32),
            pltpu.VMEM((N_TP, 8, 128), i32),
            pltpu.VMEM((8, 128), i32),
            pltpu.VMEM((2, 8, 128), i32),
            pltpu.VMEM((SESS, 32, HD), f32),
            pltpu.VMEM((SESS, 2, 8, HD), f32),
            pltpu.VMEM((SESS, 32, HD), bf16),
            pltpu.VMEM((2, SESS, 32, HD), bf16),
            pltpu.VMEM((SESS, 16, HD), f32),
            pltpu.VMEM((N_TP, SESS, 16, HD), bf16),
            pltpu.VMEM((N_TP, SESS + 1, 16, HD), f32),
            pltpu.VMEM((N_TP, SESS + 1, 16, HD), f32),
            pltpu.VMEM((SESS, 16, HD), f32),
            pltpu.VMEM((2, SESS, 16, HD), bf16),
            pltpu.VMEM((2, SESS, 16, HD), bf16),
            dma((SLOTS,)),
            dma((N_TP,)), dma((N_TP,)),
            dma((6,)), dma((6,)),
            dma((N_TP,)), dma((N_TP,)),
            dma((N_TP,)), dma((N_TP,)),
            dma((2,)), dma((2,)),
            dma((2, NCH + NBIG)), dma((2, NCH + NBIG)),
            dma((NCH,)), dma((NCH,)),
            dma((NCH,)),
        ],
        compiler_params=pltpu.CompilerParams(
            collective_id=1, has_side_effects=True, vmem_limit_bytes=56 * 1024 * 1024
        ),
    )(ft, n1, moves, ft, st, first_query, second_query, first_fresh, second_fresh, cache)


def assemble_kernel(
    came, ft, st, n1, n2, fresh1, fresh2, rows, cache, recv, first_out, second_out, out,
    buf, in_sem, out_sem,
):
    low = lax.axis_index("tp") * SLOTS
    targets = [came[r, 4 + 2 * r + c, 0] for r in range(2) for c in range(2)]
    for n, target in enumerate(targets):
        @pl.when(target >= 0)
        def _():
            pltpu.make_async_copy(
                recv.at[n // 2, pl.ds((n % 2) * 16, 16)], buf.at[target], in_sem.at[target]
            ).start()
    for l in range(SLOTS):
        hit = functools.reduce(jnp.logical_or, [target == l for target in targets])

        @pl.when(jnp.logical_not(hit))
        def _():
            pltpu.make_async_copy(cache.at[l], buf.at[l], in_sem.at[l]).start()
    for h in range(KVH):
        first_out[:, h * HD : (h + 1) * HD] = rows[:, h, :].astype(first_out.dtype)
        second_out[:, h * HD : (h + 1) * HD] = rows[:, 8 + h, :].astype(second_out.dtype)
    for l in range(SLOTS):
        pltpu.make_async_copy(cache.at[l], buf.at[l], in_sem.at[l]).wait()
    for tables, lengths, fresh in ((ft, n1, fresh1), (st, n2, fresh2)):
        for s in range(SESS):
            slot = tables[s, lengths[s] // PAGE] - low
            row = lengths[s] % PAGE

            @pl.when((slot >= 0) & (slot < SLOTS))
            def _():
                start = pl.multiple_of((row // 16) * 16, 16)
                put = iota((16, HD), 0) == row - start
                token = fresh[s].astype(jnp.float32)
                for n in range(16):
                    new = token[n // 8 : n // 8 + 1, (n % 8) * HD : (n % 8 + 1) * HD]
                    tile = buf[slot, n, pl.ds(start, 16), :].astype(jnp.float32)
                    buf[slot, n, pl.ds(start, 16), :] = jnp.where(put, new, tile).astype(jnp.bfloat16)
    outs = [pltpu.make_async_copy(buf.at[l], out.at[l], out_sem.at[l]) for l in range(SLOTS)]
    for copy in outs:
        copy.start()
    for copy in outs:
        copy.wait()


def assemble(came, ft, st, n1, n2, fresh1, fresh2, rows, cache, recv):
    vmem = pl.BlockSpec(memory_space=pltpu.VMEM)
    hbm = pl.BlockSpec(memory_space=pl.ANY)
    smem = pl.BlockSpec(memory_space=pltpu.SMEM)
    flat = jax.ShapeDtypeStruct((SESS, 8 * HD), jnp.bfloat16)
    return pl.pallas_call(
        assemble_kernel,
        name="assemble",
        out_shape=(flat, flat, jax.ShapeDtypeStruct(cache.shape, cache.dtype)),
        in_specs=[smem] * 5 + [vmem] * 3 + [hbm] * 2,
        out_specs=(vmem, vmem, hbm),
        scratch_shapes=[
            pltpu.VMEM((SLOTS, 16, PAGE, HD), jnp.bfloat16),
            pltpu.SemaphoreType.DMA((SLOTS,)),
            pltpu.SemaphoreType.DMA((SLOTS,)),
        ],
        compiler_params=pltpu.CompilerParams(vmem_limit_bytes=56 * 1024 * 1024),
    )(came, ft, st, n1, n2, fresh1, fresh2, rows, cache, recv)


def shards(
    cache_pool,
    first_query,
    second_query,
    first_fresh,
    second_fresh,
    first_tables,
    second_tables,
    first_lengths,
    second_lengths,
    page_moves,
):
    cache = cache_pool.reshape(SLOTS, 16, PAGE, HD)
    rows, recv, came = exchange(
        first_tables, first_lengths, page_moves, second_tables, first_query, second_query,
        first_fresh, second_fresh, cache,
    )
    first_out, second_out, cache_after = assemble(
        came, first_tables, second_tables, first_lengths, second_lengths, first_fresh, second_fresh,
        rows, cache, recv,
    )
    return first_out, second_out, cache_after.reshape(cache_pool.shape)


def solution(mesh):
    placed = (
        P(("inst", "tp"), None, None, None, None),
        P("inst", "tp"),
        P("inst", "tp"),
        P("inst", None, None),
        P("inst", None, None),
        P("inst", None),
        P("inst", None),
        P("inst"),
        P("inst"),
        P(("inst", "tp"), None, None, None),
    )
    return jax.shard_map(
        shards,
        mesh=mesh,
        in_specs=placed,
        out_specs=(P("inst", "tp"), P("inst", "tp"), P(("inst", "tp"), None, None, None, None)),
        check_vma=False,
    )
```

```python
import functools

import jax
import jax.numpy as jnp
from jax import lax
from jax.experimental import pallas as pl
from jax.experimental.pallas import tpu as pltpu
from jax.sharding import PartitionSpec as P

HEADS = 128
KVH = 8
HD = 128
PAGE = 128
SLOTS = 12
SESS = 4
N_INST = 8
N_TP = 16
MESH = pl.DeviceIdType.MESH
TILES = 32
CHUNK = 2
NCH = TILES // CHUNK
HALF = NCH // 2
BIG = 8
NBIG = TILES // BIG


def iota(shape, dim):
    return lax.broadcasted_iota(jnp.int32, shape, dim)


def one_hot(row):
    hot = jnp.where(iota((PAGE, HD), 0) == row, 1.0, 0.0).astype(jnp.bfloat16)
    return hot.reshape(8, 16, HD)


def spread(row):
    return jnp.broadcast_to(row, (16, HD)).astype(jnp.bfloat16)[None]


def exchange_kernel(
    ints, moves, tabs, queries, tokens, cache,
    out_ref, recv_ref, rmeta_ref, cbuf,
    pay, rel, pages, meta, metas, xtab, mine32, fr1, mine, xmine, fr2, qall, psend, prec,
    osc, xsend, xrecv,
    load_sem, m_ss, m_rs, x_ss, x_rs, q_ss, q_rs, p_ss, p_rs, o_ss, o_rs,
    g_ss, g_rs, f_ss, f_rs, r_rs,
):
    i = lax.axis_index("inst")
    t = lax.axis_index("tp")
    xh = i // 4
    y = i % 4

    def inst(h, row):
        return lax.rem(h + 2, 2) * 4 + lax.rem(row + 4, 4)

    def at(k):
        return (lax.rem(i + k + N_INST, N_INST), t)

    def peer(u):
        return lax.rem(t + u, N_TP)

    def remote(src, dst, ss, rs, dev):
        return pltpu.make_async_remote_copy(src, dst, ss, rs, device_id=dev, device_id_type=MESH)

    loads = [pltpu.make_async_copy(cache.at[l], cbuf.at[l], load_sem.at[l]) for l in range(SLOTS)]
    for load in loads:
        load.start()

    barrier = pltpu.get_barrier_semaphore()
    for u in range(1, N_TP):
        pl.semaphore_signal(barrier, 1, device_id=(i, peer(u)), device_id_type=MESH)
    for k in range(1, N_INST):
        pl.semaphore_signal(barrier, 1, device_id=at(k), device_id_type=MESH)

    low = t * SLOTS
    n1 = [ints[16, s] for s in range(SESS)]
    n2 = [ints[24, s] for s in range(SESS)]
    slots, numbers = [], []
    for s in range(SESS):
        def look(p, found, s=s):
            slot0, slot1, page0, page1 = found
            v = ints[s, p] - low
            hit = (v >= 0) & (v < SLOTS)
            new = hit & (page0 < 0)
            return (
                jnp.where(new, v, slot0), jnp.where(hit, v, slot1),
                jnp.where(new, p, page0), jnp.where(hit, p, page1),
            )

        zero, none = jnp.int32(0), jnp.int32(-1)
        slot0, slot1, page0, page1 = lax.fori_loop(0, 32, look, (zero, zero, none, none), unroll=8)
        slots += [slot0, slot1]
        numbers += [page0, page1]

    rows8 = iota((8, 128), 0)
    sources, targets = {}, {}
    table = jnp.zeros((8, 128), jnp.int32)
    for r in (1, 2):
        b = lax.rem(i + r, N_INST)
        a_code = e_code = jnp.int32(-1)
        pairs = moves[0, b]
        for c in range(2):
            a, e = pairs[c, 0], pairs[c, 1]
            sources[r, c] = a
            a_code = jnp.maximum(a_code, jnp.where(a >= 0, low + a, -1))
            e_code = jnp.maximum(e_code, jnp.where(e >= 0, low + e, -1))
            table = jnp.where(rows8 == 4 + 2 * (r - 1) + c, e, table)
        table = jnp.where(rows8 == 2 * r - 2, a_code, table)
        table = jnp.where(rows8 == 2 * r - 1, e_code, table)
    meta[...] = table
    for h in range(KVH):
        part = queries[:, h * HD : (h + 1) * HD].astype(jnp.float32)
        mine32[:, h, :] = part[:SESS]
        mine32[:, 8 + h, :] = part[SESS:]
    for s in range(SESS):
        first = tokens[s].astype(jnp.float32)
        second = tokens[SESS + s].astype(jnp.float32)
        for h in range(KVH):
            fr1[s, :, h, :] = first[:, h * HD : (h + 1) * HD]
            for row in range(2):
                mine32[s, 16 + 8 * row + h, :] = second[row, h * HD : (h + 1) * HD]
    for s in range(SESS):
        mine[s] = mine32[s].astype(jnp.bfloat16)

    for load in loads:
        load.wait()

    def make_pay(r):
        for c in range(2):
            slot = jnp.maximum(sources[r, c], 0)
            sess = row = jnp.int32(0)
            for e in range(2 * SESS):
                mine_is = slots[e] == slot
                sess = jnp.where(mine_is, e // 2, sess)
                row = jnp.where(mine_is, n1[e // 2] - numbers[e] * PAGE, row)
            hot = one_hot(row)
            keep = 1 - hot

            def one(n, carry, slot=slot, sess=sess, hot=hot, keep=keep, c=c):
                fresh = spread(fr1[sess, n // 8, pl.ds(n % 8, 1), :])
                tile = cbuf[slot, n].reshape(8, 16, HD) * keep + fresh * hot
                pay[r - 1, c * 16 + n] = tile.reshape(PAGE, HD)
                return carry

            lax.fori_loop(0, 16, one, 0, unroll=4)

    make_pay(1)
    make_pay(2)
    pl.semaphore_wait(barrier, N_TP + N_INST - 2)

    def meta_copy(u):
        return remote(meta, metas.at[t], m_ss.at[u], m_rs.at[t], (i, peer(u)))

    for u in range(1, N_TP):
        meta_copy(u).start()
    cross = []
    for r in (1, 2):
        cross.append(remote(mine, xmine.at[r - 1], x_ss.at[r - 1], x_rs.at[r - 1], at(-r)))
        cross.append(remote(tabs.at[pl.ds(8, 8)], xtab.at[r - 1], x_ss.at[1 + r], x_rs.at[1 + r], at(-r)))
        cross.append(remote(meta, rmeta_ref.at[r - 1], x_ss.at[3 + r], x_rs.at[3 + r], at(r)))
    for copy in cross:
        copy.start()

    def chunk(k):
        return pl.ds(k * CHUNK, CHUNK)

    to_relay = {1: (inst(xh, y + 1), t), 2: (inst(xh, y - 1), t)}

    def direct(r, q):
        tiles = pl.ds(q * BIG, BIG)
        return remote(
            pay.at[r - 1, tiles], recv_ref.at[r - 1, tiles],
            g_ss.at[r - 1, NCH + q], g_rs.at[r - 1, NCH + q], at(r),
        )

    def first_leg(r, k):
        return remote(
            pay.at[r - 1, chunk(k)], rel.at[chunk(k)], g_ss.at[r - 1, k], r_rs.at[k], to_relay[r]
        )

    forward_to = {1: (inst(xh + 1, y), t), 2: (inst(xh + jnp.where(y == 1, 1, 0), y - 1), t)}

    def second_leg(r, k):
        return remote(
            rel.at[chunk(k)], recv_ref.at[r - 1, chunk(k)], f_ss.at[k], g_rs.at[r - 1, k], forward_to[r]
        )

    def each(low, high, fn):
        def body(k, carry):
            fn(k)
            return carry

        lax.fori_loop(low, high, body, 0)

    even = y % 2 == 0
    odd = y % 2 == 1
    last = y == 3
    @pl.when(even)
    def _():
        each(0, HALF, lambda k: first_leg(2, k).start())

    @pl.when(last)
    def _():
        each(0, NCH, lambda k: first_leg(1, k).start())

    @pl.when(y < 3)
    def _():
        each(0, NBIG, lambda q: direct(1, q).start())

    def relay_one(low, high):
        @pl.when(y == 0)
        def _():
            def step(k):
                first_leg(1, k).wait_recv()
                second_leg(1, k).start()

            each(low, high, step)

    def relay_two(low, high):
        @pl.when(odd)
        def _():
            def step(k):
                first_leg(2, k).wait_recv()
                second_leg(2, k).start()

            each(low, high, step)

    for u in range(1, N_TP):
        remote(meta, metas.at[peer(u)], m_ss.at[u], m_rs.at[peer(u)], (i, peer(u))).wait_recv()
    for copy in cross:
        copy.wait_recv()
    codes = meta[...]
    for u in range(1, N_TP):
        codes = jnp.maximum(codes, metas[peer(u)])
    left = []
    arrives = []
    for r in (1, 2):
        a_code = codes[2 * r - 2 : 2 * r - 1, :]
        e_code = codes[2 * r - 1 : 2 * r, :]
        left.append(jnp.minimum(jnp.max(jnp.where(tabs[0:8, :] == a_code, rows8, 0)), SESS - 1))
        arrives.append(jnp.minimum(jnp.max(jnp.where(xtab[r - 1] == e_code, rows8, 0)), SESS - 1))


    relay_two(0, 2)
    relay_one(0, 2)
    lower = iota((16, 128), 0) >= 8
    for s in range(SESS):
        own = mine[s].astype(jnp.float32)
        query = own[:16]
        fresh = own[16:]
        for r in (0, 1):
            other = xmine[r, arrives[r]].astype(jnp.float32)
            hit = jnp.where(left[r] == s, 1, 0)
            query = jnp.where(lower & (hit == 1), other[:16], query)
            fresh = jnp.where(hit == 1, other[16:], fresh)
        qall[t, s] = query.astype(jnp.bfloat16)
        fr2[s] = fresh

    def q_copy(u):
        return remote(qall.at[t], qall.at[t], q_ss.at[u], q_rs.at[t], (i, peer(u)))

    for u in range(1, N_TP):
        q_copy(u).start()

    for s in range(SESS):
        for j in range(2):
            e = s * 2 + j
            slot = slots[e]
            row1 = n1[s] - numbers[e] * PAGE
            hot1 = one_hot(row1)
            hot2 = one_hot(row1 + 1)
            keep = 1 - hot1 - hot2

            def one(n, carry, slot=slot, hot1=hot1, hot2=hot2, keep=keep, s=s, e=e):
                fresh1 = spread(fr1[s, n // 8, pl.ds(n % 8, 1), :])
                fresh2 = spread(fr2[s, pl.ds(n, 1), :])
                tile = cbuf[slot, n].reshape(8, 16, HD) * keep + fresh1 * hot1 + fresh2 * hot2
                pages[e, n] = tile.reshape(PAGE, HD)
                return carry

            lax.fori_loop(0, 16, one, 0, unroll=4)

    relay_two(2, 4)
    relay_one(2, 4)
    for u in range(1, N_TP):
        remote(
            qall.at[t], qall.at[peer(u)], q_ss.at[u], q_rs.at[peer(u)], (i, peer(u))
        ).wait_recv()


    relay_two(4, 6)
    relay_one(4, 6)
    lane = iota((32, 128), 1)
    step_two = (iota((32, 128), 0) // 8) % 2
    lane_group = lane // 16

    def p_copy(dst):
        return remote(psend.at[dst], prec.at[t], p_ss.at[dst], p_rs.at[t], (i, dst))

    def head_step(kk, carry):
        k = lax.rem(kk + t // 2 + 1, KVH)
        stat = jnp.zeros((32, 128), jnp.float32)
        for s in range(SESS):
            query = qall[pl.ds(2 * k, 2), s].reshape(32, HD)
            keys = pages[pl.ds(2 * s, 2), k].reshape(2 * PAGE, HD)
            both = lax.dot_general(
                query, keys, (((1,), (1,)), ((), ())), preferred_element_type=jnp.float32
            ) * (HD ** -0.5)
            tops, totals, sums = [], [], []
            for j in range(2):
                e = s * 2 + j
                scores = both[:, j * PAGE : (j + 1) * PAGE]
                visible = lane + numbers[e] * PAGE <= n1[s] + step_two
                top = jnp.max(jnp.where(visible, scores, -1e30), axis=1, keepdims=True)
                weight = jnp.where(visible, jnp.exp(scores - top), 0.0)
                tops.append(top)
                totals.append(jnp.sum(weight, axis=1, keepdims=True))
                sums.append(
                    jnp.dot(
                        weight.astype(jnp.bfloat16), pages[e, KVH + k],
                        preferred_element_type=jnp.float32,
                    )
                )
            top = jnp.maximum(tops[0], tops[1])
            f0 = jnp.exp(tops[0] - top)
            f1 = jnp.exp(tops[1] - top)
            psend[pl.ds(2 * k, 2), s] = (f0 * sums[0] + f1 * sums[1]).reshape(2, 16, HD)
            stat = jnp.where(lane_group == 2 * s, top, stat)
            stat = jnp.where(lane_group == 2 * s + 1, f0 * totals[0] + f1 * totals[1], stat)
        psend[pl.ds(2 * k, 2), SESS] = stat.reshape(2, 16, HD)
        for d in range(2):
            @pl.when(2 * k + d != t)
            def _():
                p_copy(2 * k + d).start()
        relay_two(6 + kk * 2 // 8, 6 + (kk + 1) * 2 // 8)

        @pl.when(odd & (kk == 7))
        def _():
            each(0, NBIG, lambda q: direct(2, q).start())

        return carry

    lax.fori_loop(0, KVH, head_step, 0)

    relay_one(6, 10)
    for u in range(1, N_TP):
        remote(
            psend.at[t], prec.at[peer(u)], p_ss.at[t], p_rs.at[peer(u)], (i, peer(u))
        ).wait_recv()
    prec[t] = psend[t]
    relay_one(10, 14)
    def top_step(u, best):
        return jnp.maximum(best, prec[u, SESS])

    best = lax.fori_loop(1, N_TP, top_step, prec[0, SESS])

    def sum_step(u, carry):
        acc, tot = carry
        stat = prec[u, SESS]
        factor = jnp.exp(stat - best)
        new_acc = []
        new_tot = []
        for s in range(SESS):
            f = factor[:, 32 * s : 32 * s + 1]
            new_acc.append(acc[s] + f * prec[u, s])
            new_tot.append(tot[s] + f * stat[:, 32 * s + 16 : 32 * s + 17])
        return tuple(new_acc), tuple(new_tot)

    zero = jnp.zeros((16, HD), jnp.float32)
    none = jnp.zeros((16, 1), jnp.float32)
    acc, tot = lax.fori_loop(0, N_TP, sum_step, ((zero,) * SESS, (none,) * SESS))
    for s in range(SESS):
        osc[s] = acc[s] / tot[s]

    relay_one(14, 16)

    @pl.when(last)
    def _():
        each(0, NCH, lambda k: first_leg(1, k).wait_send())

    @pl.when(y < 3)
    def _():
        each(0, NBIG, lambda q: direct(1, q).wait_send())

    @pl.when(even)
    def _():
        each(NBIG // 2, NBIG, lambda q: direct(2, q).start())

    for r in (0, 1):
        row = osc[left[r]]
        for s in range(SESS):
            xsend[r, s] = jnp.where(arrives[r] == s, row, 0.0).astype(jnp.bfloat16)
    outs = [remote(xsend.at[r], xrecv.at[r], o_ss.at[r], o_rs.at[r], at(r + 1)) for r in (0, 1)]
    for copy in outs:
        copy.start()
    places = []
    for step, lengths in enumerate((n1, n2)):
        for s in range(SESS):
            places.append((ints[8 * step + s, lengths[s] // PAGE] - low, lengths[s] % PAGE))
    for l in range(SLOTS):
        marks = []
        for step in range(2):
            sess, row = jnp.int32(0), jnp.int32(-1)
            for s in range(SESS):
                slot, at_row = places[step * SESS + s]
                sess = jnp.where(slot == l, s, sess)
                row = jnp.where(slot == l, at_row, row)
            marks.append((sess, one_hot(row)))
        (sess1, hot1), (sess2, hot2) = marks
        keep = 1 - hot1 - hot2

        def one(n, carry, l=l, sess1=sess1, sess2=sess2, hot1=hot1, hot2=hot2, keep=keep):
            token1 = spread(fr1[sess1, n // 8, pl.ds(n % 8, 1), :])
            token2 = spread(mine32[sess2, pl.ds(16 + n, 1), :])
            tile = cbuf[l, n].reshape(8, 16, HD) * keep + token1 * hot1 + token2 * hot2
            cbuf[l, n] = tile.reshape(PAGE, HD)
            return carry

        lax.fori_loop(0, 16, one, 0, unroll=4)
    for copy in outs:
        copy.wait_recv()
    for s in range(SESS):
        gone = jnp.where((left[0] == s) | (left[1] == s), 1, 0)
        came = xrecv[0, s].astype(jnp.float32) + xrecv[1, s].astype(jnp.float32)
        out_ref[s] = jnp.where(lower & (gone == 1), came, osc[s])

    for u in range(1, N_TP):
        meta_copy(u).wait_send()
        q_copy(u).wait_send()
        p_copy(peer(u)).wait_send()
    for copy in cross + outs:
        copy.wait_send()
    @pl.when(y == 0)
    def _():
        each(0, NCH, lambda k: second_leg(1, k).wait_send())

    @pl.when(odd)
    def _():
        each(0, HALF, lambda k: second_leg(2, k).wait_send())
        each(0, NBIG, lambda q: direct(2, q).wait_send())

    @pl.when(even)
    def _():
        each(0, HALF, lambda k: first_leg(2, k).wait_send())
        each(NBIG // 2, NBIG, lambda q: direct(2, q).wait_send())

    @pl.when(y == 0)
    def _():
        each(0, NCH, lambda k: second_leg(1, k).wait_recv())

    @pl.when(y > 0)
    def _():
        each(0, NBIG, lambda q: direct(1, q).wait_recv())

    @pl.when(odd)
    def _():
        each(0, NBIG, lambda q: direct(2, q).wait_recv())

    @pl.when(even)
    def _():
        each(0, HALF, lambda k: second_leg(2, k).wait_recv())
        each(NBIG // 2, NBIG, lambda q: direct(2, q).wait_recv())


def exchange(ints, moves, queries, tokens, cache):
    vmem = pl.BlockSpec(memory_space=pltpu.VMEM)
    smem = pl.BlockSpec(memory_space=pltpu.SMEM)
    hbm = pl.BlockSpec(memory_space=pl.ANY)
    dma = pltpu.SemaphoreType.DMA
    bf16, f32, i32 = jnp.bfloat16, jnp.float32, jnp.int32
    return pl.pallas_call(
        exchange_kernel,
        name="exchange",
        out_shape=(
            jax.ShapeDtypeStruct((SESS, 16, HD), f32),
            jax.ShapeDtypeStruct((2, TILES, PAGE, HD), bf16),
            jax.ShapeDtypeStruct((2, 8, 128), i32),
            jax.ShapeDtypeStruct((SLOTS, 16, PAGE, HD), bf16),
        ),
        in_specs=[smem, vmem, vmem, vmem, vmem, hbm],
        out_specs=(vmem, hbm, vmem, vmem),
        scratch_shapes=[
            pltpu.VMEM((2, TILES, PAGE, HD), bf16),
            pltpu.VMEM((TILES, PAGE, HD), bf16),
            pltpu.VMEM((2 * SESS, 16, PAGE, HD), bf16),
            pltpu.VMEM((8, 128), i32),
            pltpu.VMEM((N_TP, 8, 128), i32),
            pltpu.VMEM((2, 8, 128), i32),
            pltpu.VMEM((SESS, 32, HD), f32),
            pltpu.VMEM((SESS, 2, 8, HD), f32),
            pltpu.VMEM((SESS, 32, HD), bf16),
            pltpu.VMEM((2, SESS, 32, HD), bf16),
            pltpu.VMEM((SESS, 16, HD), f32),
            pltpu.VMEM((N_TP, SESS, 16, HD), bf16),
            pltpu.VMEM((N_TP, SESS + 1, 16, HD), f32),
            pltpu.VMEM((N_TP, SESS + 1, 16, HD), f32),
            pltpu.VMEM((SESS, 16, HD), f32),
            pltpu.VMEM((2, SESS, 16, HD), bf16),
            pltpu.VMEM((2, SESS, 16, HD), bf16),
            dma((SLOTS,)),
            dma((N_TP,)), dma((N_TP,)),
            dma((6,)), dma((6,)),
            dma((N_TP,)), dma((N_TP,)),
            dma((N_TP,)), dma((N_TP,)),
            dma((2,)), dma((2,)),
            dma((2, NCH + NBIG)), dma((2, NCH + NBIG)),
            dma((NCH,)), dma((NCH,)),
            dma((NCH,)),
        ],
        compiler_params=pltpu.CompilerParams(
            collective_id=1, has_side_effects=True, vmem_limit_bytes=44 * 1024 * 1024
        ),
    )(ints, moves, ints, queries, tokens, cache)


def assemble_kernel(came, ints, fresh, rows, kept, recv, first_out, second_out, out, buf, sem):
    low = lax.axis_index("tp") * SLOTS
    targets = [came[r, 4 + 2 * r + c, 0] for r in range(2) for c in range(2)]
    for l in range(SLOTS):
        hit = functools.reduce(jnp.logical_or, [target == l for target in targets])

        @pl.when(jnp.logical_not(hit))
        def _():
            pltpu.make_async_copy(kept.at[l], out.at[l], sem.at[l]).start()
    tokens = [fresh[SESS + s].astype(jnp.float32) for s in range(SESS)]
    n2 = [ints[24, s] for s in range(SESS)]
    for e, target in enumerate(targets):
        row = jnp.int32(-1)
        token = tokens[0]
        for s in range(SESS):
            hit = (ints[8 + s, n2[s] // PAGE] - low == target) & (target >= 0)
            row = jnp.where(hit, n2[s] % PAGE, row)
            token = jnp.where(hit, tokens[s], token)
        hot = one_hot(row)
        keep = 1 - hot
        for n in range(16):
            new = spread(token[n // 8 : n // 8 + 1, (n % 8) * HD : (n % 8 + 1) * HD])
            tile = recv[e // 2, (e % 2) * 16 + n].reshape(8, 16, HD) * keep + new * hot
            buf[e, n] = tile.reshape(PAGE, HD)

        @pl.when(target >= 0)
        def _():
            pltpu.make_async_copy(buf.at[e], out.at[target], sem.at[target]).start()
    for h in range(KVH):
        first_out[:, h * HD : (h + 1) * HD] = rows[:, h, :].astype(first_out.dtype)
        second_out[:, h * HD : (h + 1) * HD] = rows[:, 8 + h, :].astype(second_out.dtype)
    for l in range(SLOTS):
        pltpu.make_async_copy(kept.at[l], out.at[l], sem.at[l]).wait()


def assemble(came, ints, fresh, rows, kept, recv):
    vmem = pl.BlockSpec(memory_space=pltpu.VMEM)
    hbm = pl.BlockSpec(memory_space=pl.ANY)
    smem = pl.BlockSpec(memory_space=pltpu.SMEM)
    flat = jax.ShapeDtypeStruct((SESS, 8 * HD), jnp.bfloat16)
    return pl.pallas_call(
        assemble_kernel,
        name="assemble",
        out_shape=(flat, flat, jax.ShapeDtypeStruct(kept.shape, kept.dtype)),
        in_specs=[smem] * 2 + [vmem] * 2 + [hbm, vmem],
        out_specs=(vmem, vmem, hbm),
        scratch_shapes=[
            pltpu.VMEM((4, 16, PAGE, HD), jnp.bfloat16),
            pltpu.SemaphoreType.DMA((SLOTS,)),
        ],
        compiler_params=pltpu.CompilerParams(vmem_limit_bytes=16 * 1024 * 1024),
    )(came, ints, fresh, rows, kept, recv)


def shards(
    cache_pool,
    first_query,
    second_query,
    first_fresh,
    second_fresh,
    first_tables,
    second_tables,
    first_lengths,
    second_lengths,
    page_moves,
):
    cache = cache_pool.reshape(SLOTS, 16, PAGE, HD)
    edge = ((0, 4), (0, 128 - first_tables.shape[1]))
    line = ((0, 7), (0, 128 - SESS))
    ints = jnp.concatenate(
        [
            jnp.pad(first_tables, edge, constant_values=-2),
            jnp.pad(second_tables, edge, constant_values=-2),
            jnp.pad(first_lengths[None], line),
            jnp.pad(second_lengths[None], line),
        ]
    )
    queries = jnp.concatenate([first_query, second_query])
    tokens = jnp.concatenate([first_fresh, second_fresh])
    rows, recv, came, kept = exchange(ints, page_moves, queries, tokens, cache)
    first_out, second_out, cache_after = assemble(came, ints, tokens, rows, kept, recv)
    return first_out, second_out, cache_after.reshape(cache_pool.shape)


def solution(mesh):
    placed = (
        P(("inst", "tp"), None, None, None, None),
        P("inst", "tp"),
        P("inst", "tp"),
        P("inst", None, None),
        P("inst", None, None),
        P("inst", None),
        P("inst", None),
        P("inst"),
        P("inst"),
        P(("inst", "tp"), None, None, None),
    )
    return jax.shard_map(
        shards,
        mesh=mesh,
        in_specs=placed,
        out_specs=(P("inst", "tp"), P("inst", "tp"), P(("inst", "tp"), None, None, None, None)),
        check_vma=False,
    )
```

```python
import functools

import jax
import jax.numpy as jnp
from jax import lax
from jax.experimental import pallas as pl
from jax.experimental.pallas import tpu as pltpu
from jax.sharding import PartitionSpec as P

HEADS = 128
KVH = 8
HD = 128
PAGE = 128
SLOTS = 12
SESS = 4
N_INST = 8
N_TP = 16
MESH = pl.DeviceIdType.MESH
TILES = 32
CHUNK = 2
NCH = TILES // CHUNK
HALF = NCH // 2
BIG = 8
NBIG = TILES // BIG


def iota(shape, dim):
    return lax.broadcasted_iota(jnp.int32, shape, dim)


def one_hot(row):
    hot = jnp.where(iota((PAGE, HD), 0) == row, 1.0, 0.0).astype(jnp.bfloat16)
    return hot.reshape(8, 16, HD)


def spread(row):
    return jnp.broadcast_to(row, (16, HD)).astype(jnp.bfloat16)[None]


def exchange_kernel(
    ints, moves, tabs, floats, cache,
    out_ref, recv_ref, rmeta_ref, cbuf,
    pay, rel, pages, meta, metas, xtab, mine32, fr1, mine, xmine, fr2, qall, psend, prec,
    osc, xsend, xrecv,
    load_sem, m_ss, m_rs, x_ss, x_rs, q_ss, q_rs, p_ss, p_rs, o_ss, o_rs,
    g_ss, g_rs, f_ss, f_rs, r_rs,
):
    i = lax.axis_index("inst")
    t = lax.axis_index("tp")
    xh = i // 4
    y = i % 4

    def inst(h, row):
        return lax.rem(h + 2, 2) * 4 + lax.rem(row + 4, 4)

    def at(k):
        return (lax.rem(i + k + N_INST, N_INST), t)

    def peer(u):
        return lax.rem(t + u, N_TP)

    def remote(src, dst, ss, rs, dev):
        return pltpu.make_async_remote_copy(src, dst, ss, rs, device_id=dev, device_id_type=MESH)

    loads = [pltpu.make_async_copy(cache.at[l], cbuf.at[l], load_sem.at[l]) for l in range(SLOTS)]
    for load in loads:
        load.start()

    barrier = pltpu.get_barrier_semaphore()
    for u in range(1, N_TP):
        pl.semaphore_signal(barrier, 1, device_id=(i, peer(u)), device_id_type=MESH)
    for k in range(1, N_INST):
        pl.semaphore_signal(barrier, 1, device_id=at(k), device_id_type=MESH)

    low = t * SLOTS
    n1 = [ints[16, s] for s in range(SESS)]
    n2 = [ints[24, s] for s in range(SESS)]
    slots, numbers = [], []
    for s in range(SESS):
        def look(p, found, s=s):
            slot0, slot1, page0, page1 = found
            v = ints[s, p] - low
            hit = (v >= 0) & (v < SLOTS)
            new = hit & (page0 < 0)
            return (
                jnp.where(new, v, slot0), jnp.where(hit, v, slot1),
                jnp.where(new, p, page0), jnp.where(hit, p, page1),
            )

        zero, none = jnp.int32(0), jnp.int32(-1)
        slot0, slot1, page0, page1 = lax.fori_loop(0, 32, look, (zero, zero, none, none), unroll=8)
        slots += [slot0, slot1]
        numbers += [page0, page1]

    rows8 = iota((8, 128), 0)
    sources, targets = {}, {}
    table = jnp.zeros((8, 128), jnp.int32)
    for r in (1, 2):
        b = lax.rem(i + r, N_INST)
        a_code = e_code = jnp.int32(-1)
        pairs = moves[0, b]
        for c in range(2):
            a, e = pairs[c, 0], pairs[c, 1]
            sources[r, c] = a
            a_code = jnp.maximum(a_code, jnp.where(a >= 0, low + a, -1))
            e_code = jnp.maximum(e_code, jnp.where(e >= 0, low + e, -1))
            table = jnp.where(rows8 == 4 + 2 * (r - 1) + c, e, table)
        table = jnp.where(rows8 == 2 * r - 2, a_code, table)
        table = jnp.where(rows8 == 2 * r - 1, e_code, table)
    meta[...] = table
    for s in range(SESS):
        flat = floats[s].astype(jnp.float32)
        for h in range(KVH):
            part = flat[:, h * HD : (h + 1) * HD]
            for row in range(2):
                mine32[s, 8 * row + h, :] = part[row]
                fr1[s, row, h, :] = part[2 + row]
                mine32[s, 16 + 8 * row + h, :] = part[4 + row]
    for s in range(SESS):
        mine[s] = mine32[s].astype(jnp.bfloat16)

    for load in loads:
        load.wait()

    def make_pay(r):
        for c in range(2):
            slot = jnp.maximum(sources[r, c], 0)
            sess = row = jnp.int32(0)
            for e in range(2 * SESS):
                mine_is = slots[e] == slot
                sess = jnp.where(mine_is, e // 2, sess)
                row = jnp.where(mine_is, n1[e // 2] - numbers[e] * PAGE, row)
            hot = one_hot(row)
            keep = 1 - hot

            def one(n, carry, slot=slot, sess=sess, hot=hot, keep=keep, c=c):
                fresh = spread(fr1[sess, n // 8, pl.ds(n % 8, 1), :])
                tile = cbuf[slot, n].reshape(8, 16, HD) * keep + fresh * hot
                pay[r - 1, c * 16 + n] = tile.reshape(PAGE, HD)
                return carry

            lax.fori_loop(0, 16, one, 0, unroll=4)

    make_pay(1)
    make_pay(2)
    pl.semaphore_wait(barrier, N_TP + N_INST - 2)

    def meta_copy(u):
        return remote(meta, metas.at[t], m_ss.at[u], m_rs.at[t], (i, peer(u)))

    for u in range(1, N_TP):
        meta_copy(u).start()
    cross = []
    for r in (1, 2):
        cross.append(remote(mine, xmine.at[r - 1], x_ss.at[r - 1], x_rs.at[r - 1], at(-r)))
        cross.append(remote(tabs.at[pl.ds(8, 8)], xtab.at[r - 1], x_ss.at[1 + r], x_rs.at[1 + r], at(-r)))
        cross.append(remote(meta, rmeta_ref.at[r - 1], x_ss.at[3 + r], x_rs.at[3 + r], at(r)))
    for copy in cross:
        copy.start()

    def chunk(k):
        return pl.ds(k * CHUNK, CHUNK)

    to_relay = {1: (inst(xh, y + 1), t), 2: (inst(xh, y - 1), t)}

    def direct(r, q):
        tiles = pl.ds(q * BIG, BIG)
        return remote(
            pay.at[r - 1, tiles], recv_ref.at[r - 1, tiles],
            g_ss.at[r - 1, NCH + q], g_rs.at[r - 1, NCH + q], at(r),
        )

    def first_leg(r, k):
        return remote(
            pay.at[r - 1, chunk(k)], rel.at[chunk(k)], g_ss.at[r - 1, k], r_rs.at[k], to_relay[r]
        )

    forward_to = {1: (inst(xh + 1, y), t), 2: (inst(xh + jnp.where(y == 1, 1, 0), y - 1), t)}

    def second_leg(r, k):
        return remote(
            rel.at[chunk(k)], recv_ref.at[r - 1, chunk(k)], f_ss.at[k], g_rs.at[r - 1, k], forward_to[r]
        )

    def each(low, high, fn):
        def body(k, carry):
            fn(k)
            return carry

        lax.fori_loop(low, high, body, 0)

    even = y % 2 == 0
    odd = y % 2 == 1
    last = y == 3
    @pl.when(even)
    def _():
        each(0, HALF, lambda k: first_leg(2, k).start())

    @pl.when(last)
    def _():
        each(0, NCH, lambda k: first_leg(1, k).start())

    @pl.when(y < 3)
    def _():
        each(0, NBIG, lambda q: direct(1, q).start())

    def relay_one(low, high):
        @pl.when(y == 0)
        def _():
            def step(k):
                first_leg(1, k).wait_recv()
                second_leg(1, k).start()

            each(low, high, step)

    def relay_two(low, high):
        @pl.when(odd)
        def _():
            def step(k):
                first_leg(2, k).wait_recv()
                second_leg(2, k).start()

            each(low, high, step)

    for u in range(1, N_TP):
        remote(meta, metas.at[peer(u)], m_ss.at[u], m_rs.at[peer(u)], (i, peer(u))).wait_recv()
    for copy in cross:
        copy.wait_recv()
    codes = meta[...]
    for u in range(1, N_TP):
        codes = jnp.maximum(codes, metas[peer(u)])
    left = []
    arrives = []
    for r in (1, 2):
        a_code = codes[2 * r - 2 : 2 * r - 1, :]
        e_code = codes[2 * r - 1 : 2 * r, :]
        left.append(jnp.minimum(jnp.max(jnp.where(tabs[0:8, :] == a_code, rows8, 0)), SESS - 1))
        arrives.append(jnp.minimum(jnp.max(jnp.where(xtab[r - 1] == e_code, rows8, 0)), SESS - 1))


    relay_two(0, 2)
    relay_one(0, 2)
    lower = iota((16, 128), 0) >= 8
    for s in range(SESS):
        own = mine[s].astype(jnp.float32)
        query = own[:16]
        fresh = own[16:]
        for r in (0, 1):
            other = xmine[r, arrives[r]].astype(jnp.float32)
            hit = jnp.where(left[r] == s, 1, 0)
            query = jnp.where(lower & (hit == 1), other[:16], query)
            fresh = jnp.where(hit == 1, other[16:], fresh)
        qall[t, s] = query.astype(jnp.bfloat16)
        fr2[s] = fresh

    def q_copy(u):
        return remote(qall.at[t], qall.at[t], q_ss.at[u], q_rs.at[t], (i, peer(u)))

    for u in range(1, N_TP):
        q_copy(u).start()


    @pl.when(odd)
    def _():
        each(0, 1, lambda q: direct(2, q).start())

    for s in range(SESS):
        for j in range(2):
            e = s * 2 + j
            slot = slots[e]
            row1 = n1[s] - numbers[e] * PAGE
            hot1 = one_hot(row1)
            hot2 = one_hot(row1 + 1)
            keep = 1 - hot1 - hot2

            def one(n, carry, slot=slot, hot1=hot1, hot2=hot2, keep=keep, s=s, e=e):
                fresh1 = spread(fr1[s, n // 8, pl.ds(n % 8, 1), :])
                fresh2 = spread(fr2[s, pl.ds(n, 1), :])
                tile = cbuf[slot, n].reshape(8, 16, HD) * keep + fresh1 * hot1 + fresh2 * hot2
                pages[e, n] = tile.reshape(PAGE, HD)
                return carry

            lax.fori_loop(0, 16, one, 0, unroll=4)

    relay_two(2, 4)
    relay_one(2, 4)
    for u in range(1, N_TP):
        remote(
            qall.at[t], qall.at[peer(u)], q_ss.at[u], q_rs.at[peer(u)], (i, peer(u))
        ).wait_recv()


    relay_two(4, 6)
    relay_one(4, 6)
    lane = iota((32, 128), 1)
    step_two = (iota((32, 128), 0) // 8) % 2
    lane_group = lane // 16

    def p_copy(dst):
        return remote(psend.at[dst], prec.at[t], p_ss.at[dst], p_rs.at[t], (i, dst))

    def head_step(kk, carry):
        k = lax.rem(kk + t // 2 + 1, KVH)
        stat = jnp.zeros((32, 128), jnp.float32)
        for s in range(SESS):
            query = qall[pl.ds(2 * k, 2), s].reshape(32, HD)
            keys = pages[pl.ds(2 * s, 2), k].reshape(2 * PAGE, HD)
            both = lax.dot_general(
                query, keys, (((1,), (1,)), ((), ())), preferred_element_type=jnp.float32
            ) * (HD ** -0.5)
            tops, totals, sums = [], [], []
            for j in range(2):
                e = s * 2 + j
                scores = both[:, j * PAGE : (j + 1) * PAGE]
                visible = lane + numbers[e] * PAGE <= n1[s] + step_two
                top = jnp.max(jnp.where(visible, scores, -1e30), axis=1, keepdims=True)
                weight = jnp.where(visible, jnp.exp(scores - top), 0.0)
                tops.append(top)
                totals.append(jnp.sum(weight, axis=1, keepdims=True))
                sums.append(
                    jnp.dot(
                        weight.astype(jnp.bfloat16), pages[e, KVH + k],
                        preferred_element_type=jnp.float32,
                    )
                )
            top = jnp.maximum(tops[0], tops[1])
            f0 = jnp.exp(tops[0] - top)
            f1 = jnp.exp(tops[1] - top)
            psend[pl.ds(2 * k, 2), s] = (f0 * sums[0] + f1 * sums[1]).reshape(2, 16, HD)
            stat = jnp.where(lane_group == 2 * s, top, stat)
            stat = jnp.where(lane_group == 2 * s + 1, f0 * totals[0] + f1 * totals[1], stat)
        psend[pl.ds(2 * k, 2), SESS] = stat.reshape(2, 16, HD)
        for d in range(2):
            @pl.when(2 * k + d != t)
            def _():
                p_copy(2 * k + d).start()

        relay_two(6 + kk * 2 // 8, 6 + (kk + 1) * 2 // 8)

        @pl.when(odd & (kk == 7))
        def _():
            each(1, 4, lambda q: direct(2, q).start())

        return carry

    lax.fori_loop(0, KVH, head_step, 0)

    relay_one(6, 10)
    for u in range(1, N_TP):
        remote(
            psend.at[t], prec.at[peer(u)], p_ss.at[t], p_rs.at[peer(u)], (i, peer(u))
        ).wait_recv()
    prec[t] = psend[t]
    relay_one(10, 14)
    def top_step(u, best):
        return jnp.maximum(best, prec[u, SESS])

    best = lax.fori_loop(1, N_TP, top_step, prec[0, SESS])

    def sum_step(u, carry):
        acc, tot = carry
        stat = prec[u, SESS]
        factor = jnp.exp(stat - best)
        new_acc = []
        new_tot = []
        for s in range(SESS):
            f = factor[:, 32 * s : 32 * s + 1]
            new_acc.append(acc[s] + f * prec[u, s])
            new_tot.append(tot[s] + f * stat[:, 32 * s + 16 : 32 * s + 17])
        return tuple(new_acc), tuple(new_tot)

    zero = jnp.zeros((16, HD), jnp.float32)
    none = jnp.zeros((16, 1), jnp.float32)
    acc, tot = lax.fori_loop(0, N_TP, sum_step, ((zero,) * SESS, (none,) * SESS))
    for s in range(SESS):
        osc[s] = acc[s] / tot[s]


    relay_one(14, 16)
    for r in (0, 1):
        row = osc[left[r]]
        for s in range(SESS):
            xsend[r, s] = jnp.where(arrives[r] == s, row, 0.0).astype(jnp.bfloat16)
    outs = [remote(xsend.at[r], xrecv.at[r], o_ss.at[r], o_rs.at[r], at(r + 1)) for r in (0, 1)]
    for copy in outs:
        copy.start()

    @pl.when(last)
    def _():
        each(0, NCH, lambda k: first_leg(1, k).wait_send())

    @pl.when(y < 3)
    def _():
        each(0, NBIG, lambda q: direct(1, q).wait_send())

    @pl.when(even)
    def _():
        each(NBIG // 2, NBIG, lambda q: direct(2, q).start())

    places = []
    for step, lengths in enumerate((n1, n2)):
        for s in range(SESS):
            places.append((ints[8 * step + s, lengths[s] // PAGE] - low, lengths[s] % PAGE))
    for l in range(SLOTS):
        marks = []
        for step in range(2):
            sess, row = jnp.int32(0), jnp.int32(-1)
            for s in range(SESS):
                slot, at_row = places[step * SESS + s]
                sess = jnp.where(slot == l, s, sess)
                row = jnp.where(slot == l, at_row, row)
            marks.append((sess, one_hot(row)))
        (sess1, hot1), (sess2, hot2) = marks
        keep = 1 - hot1 - hot2

        def one(n, carry, l=l, sess1=sess1, sess2=sess2, hot1=hot1, hot2=hot2, keep=keep):
            token1 = spread(fr1[sess1, n // 8, pl.ds(n % 8, 1), :])
            token2 = spread(mine32[sess2, pl.ds(16 + n, 1), :])
            tile = cbuf[l, n].reshape(8, 16, HD) * keep + token1 * hot1 + token2 * hot2
            cbuf[l, n] = tile.reshape(PAGE, HD)
            return carry

        lax.fori_loop(0, 16, one, 0, unroll=4)
    for copy in outs:
        copy.wait_recv()
    for s in range(SESS):
        gone = jnp.where((left[0] == s) | (left[1] == s), 1, 0)
        came = xrecv[0, s].astype(jnp.float32) + xrecv[1, s].astype(jnp.float32)
        out_ref[s] = jnp.where(lower & (gone == 1), came, osc[s])

    for u in range(1, N_TP):
        meta_copy(u).wait_send()
        q_copy(u).wait_send()
        p_copy(peer(u)).wait_send()
    for copy in cross + outs:
        copy.wait_send()
    @pl.when(y == 0)
    def _():
        each(0, NCH, lambda k: second_leg(1, k).wait_send())

    @pl.when(odd)
    def _():
        each(0, HALF, lambda k: second_leg(2, k).wait_send())
        each(0, NBIG, lambda q: direct(2, q).wait_send())

    @pl.when(even)
    def _():
        each(0, HALF, lambda k: first_leg(2, k).wait_send())
        each(NBIG // 2, NBIG, lambda q: direct(2, q).wait_send())

    @pl.when(y == 0)
    def _():
        each(0, NCH, lambda k: second_leg(1, k).wait_recv())

    @pl.when(y > 0)
    def _():
        each(0, NBIG, lambda q: direct(1, q).wait_recv())

    @pl.when(odd)
    def _():
        each(0, NBIG, lambda q: direct(2, q).wait_recv())

    @pl.when(even)
    def _():
        each(0, HALF, lambda k: second_leg(2, k).wait_recv())
        each(NBIG // 2, NBIG, lambda q: direct(2, q).wait_recv())


def exchange(ints, moves, floats, cache):
    vmem = pl.BlockSpec(memory_space=pltpu.VMEM)
    smem = pl.BlockSpec(memory_space=pltpu.SMEM)
    hbm = pl.BlockSpec(memory_space=pl.ANY)
    dma = pltpu.SemaphoreType.DMA
    bf16, f32, i32 = jnp.bfloat16, jnp.float32, jnp.int32
    return pl.pallas_call(
        exchange_kernel,
        name="exchange",
        out_shape=(
            jax.ShapeDtypeStruct((SESS, 16, HD), f32),
            jax.ShapeDtypeStruct((2, TILES, PAGE, HD), bf16),
            jax.ShapeDtypeStruct((2, 8, 128), i32),
            jax.ShapeDtypeStruct((SLOTS, 16, PAGE, HD), bf16),
        ),
        in_specs=[smem, vmem, vmem, vmem, hbm],
        out_specs=(vmem, hbm, vmem, vmem),
        scratch_shapes=[
            pltpu.VMEM((2, TILES, PAGE, HD), bf16),
            pltpu.VMEM((TILES, PAGE, HD), bf16),
            pltpu.VMEM((2 * SESS, 16, PAGE, HD), bf16),
            pltpu.VMEM((8, 128), i32),
            pltpu.VMEM((N_TP, 8, 128), i32),
            pltpu.VMEM((2, 8, 128), i32),
            pltpu.VMEM((SESS, 32, HD), f32),
            pltpu.VMEM((SESS, 2, 8, HD), f32),
            pltpu.VMEM((SESS, 32, HD), bf16),
            pltpu.VMEM((2, SESS, 32, HD), bf16),
            pltpu.VMEM((SESS, 16, HD), f32),
            pltpu.VMEM((N_TP, SESS, 16, HD), bf16),
            pltpu.VMEM((N_TP, SESS + 1, 16, HD), f32),
            pltpu.VMEM((N_TP, SESS + 1, 16, HD), f32),
            pltpu.VMEM((SESS, 16, HD), f32),
            pltpu.VMEM((2, SESS, 16, HD), bf16),
            pltpu.VMEM((2, SESS, 16, HD), bf16),
            dma((SLOTS,)),
            dma((N_TP,)), dma((N_TP,)),
            dma((6,)), dma((6,)),
            dma((N_TP,)), dma((N_TP,)),
            dma((N_TP,)), dma((N_TP,)),
            dma((2,)), dma((2,)),
            dma((2, NCH + NBIG)), dma((2, NCH + NBIG)),
            dma((NCH,)), dma((NCH,)),
            dma((NCH,)),
        ],
        compiler_params=pltpu.CompilerParams(
            collective_id=1, has_side_effects=True, vmem_limit_bytes=44 * 1024 * 1024
        ),
    )(ints, moves, ints, floats, cache)


def assemble_kernel(came, ints, floats, rows, kept, recv, first_out, second_out, out, buf, sem):
    low = lax.axis_index("tp") * SLOTS
    targets = [came[r, 4 + 2 * r + c, 0] for r in range(2) for c in range(2)]
    for l in range(SLOTS):
        hit = functools.reduce(jnp.logical_or, [target == l for target in targets])

        @pl.when(jnp.logical_not(hit))
        def _():
            pltpu.make_async_copy(kept.at[l], out.at[l], sem.at[l]).start()
    tokens = [floats[s, 4:6].astype(jnp.float32) for s in range(SESS)]
    n2 = [ints[24, s] for s in range(SESS)]
    for e, target in enumerate(targets):
        row = jnp.int32(-1)
        token = tokens[0]
        for s in range(SESS):
            hit = (ints[8 + s, n2[s] // PAGE] - low == target) & (target >= 0)
            row = jnp.where(hit, n2[s] % PAGE, row)
            token = jnp.where(hit, tokens[s], token)
        hot = one_hot(row)
        keep = 1 - hot
        for n in range(16):
            new = spread(token[n // 8 : n // 8 + 1, (n % 8) * HD : (n % 8 + 1) * HD])
            tile = recv[e // 2, (e % 2) * 16 + n].reshape(8, 16, HD) * keep + new * hot
            buf[e, n] = tile.reshape(PAGE, HD)

        @pl.when(target >= 0)
        def _():
            pltpu.make_async_copy(buf.at[e], out.at[target], sem.at[target]).start()
    for h in range(KVH):
        first_out[:, h * HD : (h + 1) * HD] = rows[:, h, :].astype(first_out.dtype)
        second_out[:, h * HD : (h + 1) * HD] = rows[:, 8 + h, :].astype(second_out.dtype)
    for l in range(SLOTS):
        pltpu.make_async_copy(kept.at[l], out.at[l], sem.at[l]).wait()


def assemble(came, ints, floats, rows, kept, recv):
    vmem = pl.BlockSpec(memory_space=pltpu.VMEM)
    hbm = pl.BlockSpec(memory_space=pl.ANY)
    smem = pl.BlockSpec(memory_space=pltpu.SMEM)
    flat = jax.ShapeDtypeStruct((SESS, 8 * HD), jnp.bfloat16)
    return pl.pallas_call(
        assemble_kernel,
        name="assemble",
        out_shape=(flat, flat, jax.ShapeDtypeStruct(kept.shape, kept.dtype)),
        in_specs=[smem] * 2 + [vmem] * 2 + [hbm, vmem],
        out_specs=(vmem, vmem, hbm),
        scratch_shapes=[
            pltpu.VMEM((4, 16, PAGE, HD), jnp.bfloat16),
            pltpu.SemaphoreType.DMA((SLOTS,)),
        ],
        compiler_params=pltpu.CompilerParams(vmem_limit_bytes=16 * 1024 * 1024),
    )(came, ints, floats, rows, kept, recv)


def shards(
    cache_pool,
    first_query,
    second_query,
    first_fresh,
    second_fresh,
    first_tables,
    second_tables,
    first_lengths,
    second_lengths,
    page_moves,
):
    cache = cache_pool.reshape(SLOTS, 16, PAGE, HD)
    edge = ((0, 4), (0, 128 - first_tables.shape[1]))
    line = ((0, 7), (0, 128 - SESS))
    ints = jnp.concatenate(
        [
            jnp.pad(first_tables, edge, constant_values=-2),
            jnp.pad(second_tables, edge, constant_values=-2),
            jnp.pad(first_lengths[None], line),
            jnp.pad(second_lengths[None], line),
        ]
    )
    shape = (SESS, 6, first_query.shape[1])
    kind = lax.broadcasted_iota(jnp.int32, shape, 1)
    floats = jnp.where(
        kind < 4,
        jnp.pad(first_fresh, ((0, 0), (2, 2), (0, 0))),
        jnp.pad(second_fresh, ((0, 0), (4, 0), (0, 0))),
    )
    floats = jnp.where(kind == 0, lax.broadcast_in_dim(first_query, shape, (0, 2)), floats)
    floats = jnp.where(kind == 1, lax.broadcast_in_dim(second_query, shape, (0, 2)), floats)
    rows, recv, came, kept = exchange(ints, page_moves, floats, cache)
    first_out, second_out, cache_after = assemble(came, ints, floats, rows, kept, recv)
    return first_out, second_out, cache_after.reshape(cache_pool.shape)


def solution(mesh):
    placed = (
        P(("inst", "tp"), None, None, None, None),
        P("inst", "tp"),
        P("inst", "tp"),
        P("inst", None, None),
        P("inst", None, None),
        P("inst", None),
        P("inst", None),
        P("inst"),
        P("inst"),
        P(("inst", "tp"), None, None, None),
    )
    return jax.shard_map(
        shards,
        mesh=mesh,
        in_specs=placed,
        out_specs=(P("inst", "tp"), P("inst", "tp"), P(("inst", "tp"), None, None, None, None)),
        check_vma=False,
    )
```

```python
import functools

import jax
import jax.numpy as jnp
from jax import lax
from jax.experimental import pallas as pl
from jax.experimental.pallas import tpu as pltpu
from jax.sharding import PartitionSpec as P

HEADS = 128
KVH = 8
HD = 128
PAGE = 128
SLOTS = 12
SESS = 4
N_INST = 8
N_TP = 16
MESH = pl.DeviceIdType.MESH
TILES = 32
CHUNK = 2
NCH = TILES // CHUNK
HALF = NCH // 2
BIG = 8
NBIG = TILES // BIG


def iota(shape, dim):
    return lax.broadcasted_iota(jnp.int32, shape, dim)


def one_hot(row):
    hot = jnp.where(iota((PAGE, HD), 0) == row, 1.0, 0.0).astype(jnp.bfloat16)
    return hot.reshape(8, 16, HD)


def spread(row):
    return jnp.broadcast_to(row, (16, HD)).astype(jnp.bfloat16)[None]


def exchange_kernel(
    ints, moves, tabs, floats, cache,
    out_ref, recv_ref, rmeta_ref, cbuf,
    pay, rel, pages, meta, metas, xtab, mine32, fr1, mine, xmine, fr2, qall, psend, prec,
    osc, xsend, xrecv,
    load_sem, m_ss, m_rs, x_ss, x_rs, q_ss, q_rs, p_ss, p_rs, o_ss, o_rs,
    g_ss, g_rs, f_ss, f_rs, r_rs,
):
    i = lax.axis_index("inst")
    t = lax.axis_index("tp")
    xh = i // 4
    y = i % 4

    def inst(h, row):
        return lax.rem(h + 2, 2) * 4 + lax.rem(row + 4, 4)

    def at(k):
        return (lax.rem(i + k + N_INST, N_INST), t)

    def peer(u):
        return lax.rem(t + u, N_TP)

    def remote(src, dst, ss, rs, dev):
        return pltpu.make_async_remote_copy(src, dst, ss, rs, device_id=dev, device_id_type=MESH)

    loads = [pltpu.make_async_copy(cache.at[l], cbuf.at[l], load_sem.at[l]) for l in range(SLOTS)]
    for load in loads:
        load.start()

    barrier = pltpu.get_barrier_semaphore()
    for u in range(1, N_TP):
        pl.semaphore_signal(barrier, 1, device_id=(i, peer(u)), device_id_type=MESH)
    for k in range(1, N_INST):
        pl.semaphore_signal(barrier, 1, device_id=at(k), device_id_type=MESH)

    low = t * SLOTS
    n1 = [ints[16, s] for s in range(SESS)]
    n2 = [ints[24, s] for s in range(SESS)]
    slots, numbers = [], []
    for s in range(SESS):
        def look(p, found, s=s):
            slot0, slot1, page0, page1 = found
            v = ints[s, p] - low
            hit = (v >= 0) & (v < SLOTS)
            new = hit & (page0 < 0)
            return (
                jnp.where(new, v, slot0), jnp.where(hit, v, slot1),
                jnp.where(new, p, page0), jnp.where(hit, p, page1),
            )

        zero, none = jnp.int32(0), jnp.int32(-1)
        slot0, slot1, page0, page1 = lax.fori_loop(0, 32, look, (zero, zero, none, none), unroll=8)
        slots += [slot0, slot1]
        numbers += [page0, page1]

    rows8 = iota((8, 128), 0)
    sources, targets = {}, {}
    table = jnp.zeros((8, 128), jnp.int32)
    for r in (1, 2):
        b = lax.rem(i + r, N_INST)
        a_code = e_code = jnp.int32(-1)
        pairs = moves[0, b]
        for c in range(2):
            a, e = pairs[c, 0], pairs[c, 1]
            sources[r, c] = a
            a_code = jnp.maximum(a_code, jnp.where(a >= 0, low + a, -1))
            e_code = jnp.maximum(e_code, jnp.where(e >= 0, low + e, -1))
            table = jnp.where(rows8 == 4 + 2 * (r - 1) + c, e, table)
        table = jnp.where(rows8 == 2 * r - 2, a_code, table)
        table = jnp.where(rows8 == 2 * r - 1, e_code, table)
    meta[...] = table
    for s in range(SESS):
        flat = floats[s].astype(jnp.float32)
        for h in range(KVH):
            part = flat[:, h * HD : (h + 1) * HD]
            for row in range(2):
                mine32[s, 8 * row + h, :] = part[row]
                fr1[s, row, h, :] = part[2 + row]
                mine32[s, 16 + 8 * row + h, :] = part[4 + row]
    for s in range(SESS):
        mine[s] = mine32[s].astype(jnp.bfloat16)

    for load in loads:
        load.wait()

    def make_pay(r):
        for c in range(2):
            slot = jnp.maximum(sources[r, c], 0)
            sess = row = jnp.int32(0)
            for e in range(2 * SESS):
                mine_is = slots[e] == slot
                sess = jnp.where(mine_is, e // 2, sess)
                row = jnp.where(mine_is, n1[e // 2] - numbers[e] * PAGE, row)
            hot = one_hot(row)
            keep = 1 - hot

            def one(n, carry, slot=slot, sess=sess, hot=hot, keep=keep, c=c):
                fresh = spread(fr1[sess, n // 8, pl.ds(n % 8, 1), :])
                tile = cbuf[slot, n].reshape(8, 16, HD) * keep + fresh * hot
                pay[r - 1, c * 16 + n] = tile.reshape(PAGE, HD)
                return carry

            lax.fori_loop(0, 16, one, 0, unroll=4)

    make_pay(1)
    make_pay(2)
    pl.semaphore_wait(barrier, N_TP + N_INST - 2)

    def meta_copy(u):
        return remote(meta, metas.at[t], m_ss.at[u], m_rs.at[t], (i, peer(u)))

    for u in range(1, N_TP):
        meta_copy(u).start()
    cross = []
    for r in (1, 2):
        cross.append(remote(mine, xmine.at[r - 1], x_ss.at[r - 1], x_rs.at[r - 1], at(-r)))
        cross.append(remote(tabs.at[pl.ds(8, 8)], xtab.at[r - 1], x_ss.at[1 + r], x_rs.at[1 + r], at(-r)))
        cross.append(remote(meta, rmeta_ref.at[r - 1], x_ss.at[3 + r], x_rs.at[3 + r], at(r)))
    for copy in cross:
        copy.start()

    def chunk(k):
        return pl.ds(k * CHUNK, CHUNK)

    to_relay = {1: (inst(xh, y + 1), t), 2: (inst(xh, y - 1), t)}

    def direct(r, q):
        tiles = pl.ds(q * BIG, BIG)
        return remote(
            pay.at[r - 1, tiles], recv_ref.at[r - 1, tiles],
            g_ss.at[r - 1, NCH + q], g_rs.at[r - 1, NCH + q], at(r),
        )

    def first_leg(r, k):
        return remote(
            pay.at[r - 1, chunk(k)], rel.at[chunk(k)], g_ss.at[r - 1, k], r_rs.at[k], to_relay[r]
        )

    forward_to = {1: (inst(xh + 1, y), t), 2: (inst(xh + jnp.where(y == 1, 1, 0), y - 1), t)}

    def second_leg(r, k):
        return remote(
            rel.at[chunk(k)], recv_ref.at[r - 1, chunk(k)], f_ss.at[k], g_rs.at[r - 1, k], forward_to[r]
        )

    def each(low, high, fn):
        def body(k, carry):
            fn(k)
            return carry

        lax.fori_loop(low, high, body, 0)

    even = y % 2 == 0
    odd = y % 2 == 1
    last = y == 3
    @pl.when(even)
    def _():
        each(0, HALF, lambda k: first_leg(2, k).start())

    @pl.when(last)
    def _():
        each(0, NCH, lambda k: first_leg(1, k).start())

    @pl.when(y < 3)
    def _():
        each(0, NBIG, lambda q: direct(1, q).start())

    def relay_one(low, high):
        @pl.when(y == 0)
        def _():
            def step(k):
                first_leg(1, k).wait_recv()
                second_leg(1, k).start()

            each(low, high, step)

    def relay_two(low, high):
        @pl.when(odd)
        def _():
            def step(k):
                first_leg(2, k).wait_recv()
                second_leg(2, k).start()

            each(low, high, step)

    for u in range(1, N_TP):
        remote(meta, metas.at[peer(u)], m_ss.at[u], m_rs.at[peer(u)], (i, peer(u))).wait_recv()
    for copy in cross:
        copy.wait_recv()
    codes = meta[...]
    for u in range(1, N_TP):
        codes = jnp.maximum(codes, metas[peer(u)])
    left = []
    arrives = []
    for r in (1, 2):
        a_code = codes[2 * r - 2 : 2 * r - 1, :]
        e_code = codes[2 * r - 1 : 2 * r, :]
        left.append(jnp.minimum(jnp.max(jnp.where(tabs[0:8, :] == a_code, rows8, 0)), SESS - 1))
        arrives.append(jnp.minimum(jnp.max(jnp.where(xtab[r - 1] == e_code, rows8, 0)), SESS - 1))


    relay_two(0, 2)
    relay_one(0, 2)
    lower = iota((16, 128), 0) >= 8
    for s in range(SESS):
        own = mine[s].astype(jnp.float32)
        query = own[:16]
        fresh = own[16:]
        for r in (0, 1):
            other = xmine[r, arrives[r]].astype(jnp.float32)
            hit = jnp.where(left[r] == s, 1, 0)
            query = jnp.where(lower & (hit == 1), other[:16], query)
            fresh = jnp.where(hit == 1, other[16:], fresh)
        qall[t, s] = query.astype(jnp.bfloat16)
        fr2[s] = fresh

    def q_copy(u):
        return remote(qall.at[t], qall.at[t], q_ss.at[u], q_rs.at[t], (i, peer(u)))

    for u in range(1, N_TP):
        q_copy(u).start()


    @pl.when(odd)
    def _():
        each(0, 1, lambda q: direct(2, q).start())


    @pl.when(y == 0)
    def _():
        each(2, 4, lambda q: direct(2, q).start())

    for s in range(SESS):
        for j in range(2):
            e = s * 2 + j
            slot = slots[e]
            row1 = n1[s] - numbers[e] * PAGE
            hot1 = one_hot(row1)
            hot2 = one_hot(row1 + 1)
            keep = 1 - hot1 - hot2

            def one(n, carry, slot=slot, hot1=hot1, hot2=hot2, keep=keep, s=s, e=e):
                fresh1 = spread(fr1[s, n // 8, pl.ds(n % 8, 1), :])
                fresh2 = spread(fr2[s, pl.ds(n, 1), :])
                tile = cbuf[slot, n].reshape(8, 16, HD) * keep + fresh1 * hot1 + fresh2 * hot2
                pages[e, n] = tile.reshape(PAGE, HD)
                return carry

            lax.fori_loop(0, 16, one, 0, unroll=4)

    relay_two(2, 4)
    relay_one(2, 4)
    for u in range(1, N_TP):
        remote(
            qall.at[t], qall.at[peer(u)], q_ss.at[u], q_rs.at[peer(u)], (i, peer(u))
        ).wait_recv()


    relay_two(4, 6)
    relay_one(4, 6)

    @pl.when((y == 1))
    def _():
        each(1, 2, lambda q: direct(2, q).start())

    lane = iota((32, 128), 1)
    step_two = (iota((32, 128), 0) // 8) % 2
    lane_group = lane // 16

    def p_copy(dst):
        return remote(psend.at[dst], prec.at[t], p_ss.at[dst], p_rs.at[t], (i, dst))

    def head_step(kk, carry):
        k = lax.rem(kk + t // 2 + 1, KVH)
        stat = jnp.zeros((32, 128), jnp.float32)
        for s in range(SESS):
            query = qall[pl.ds(2 * k, 2), s].reshape(32, HD)
            keys = pages[pl.ds(2 * s, 2), k].reshape(2 * PAGE, HD)
            both = lax.dot_general(
                query, keys, (((1,), (1,)), ((), ())), preferred_element_type=jnp.float32
            ) * (HD ** -0.5)
            tops, totals, sums = [], [], []
            for j in range(2):
                e = s * 2 + j
                scores = both[:, j * PAGE : (j + 1) * PAGE]
                visible = lane + numbers[e] * PAGE <= n1[s] + step_two
                top = jnp.max(jnp.where(visible, scores, -1e30), axis=1, keepdims=True)
                weight = jnp.where(visible, jnp.exp(scores - top), 0.0)
                tops.append(top)
                totals.append(jnp.sum(weight, axis=1, keepdims=True))
                sums.append(
                    jnp.dot(
                        weight.astype(jnp.bfloat16), pages[e, KVH + k],
                        preferred_element_type=jnp.float32,
                    )
                )
            top = jnp.maximum(tops[0], tops[1])
            f0 = jnp.exp(tops[0] - top)
            f1 = jnp.exp(tops[1] - top)
            psend[pl.ds(2 * k, 2), s] = (f0 * sums[0] + f1 * sums[1]).reshape(2, 16, HD)
            stat = jnp.where(lane_group == 2 * s, top, stat)
            stat = jnp.where(lane_group == 2 * s + 1, f0 * totals[0] + f1 * totals[1], stat)
        psend[pl.ds(2 * k, 2), SESS] = stat.reshape(2, 16, HD)
        for d in range(2):
            @pl.when(2 * k + d != t)
            def _():
                p_copy(2 * k + d).start()

        relay_two(6 + kk * 2 // 8, 6 + (kk + 1) * 2 // 8)

        @pl.when((y == 1) & (kk == 7))
        def _():
            each(2, 4, lambda q: direct(2, q).start())


        @pl.when((y == 3) & (kk == 7))
        def _():
            each(1, 4, lambda q: direct(2, q).start())

        return carry

    lax.fori_loop(0, KVH, head_step, 0)

    relay_one(6, 10)
    for u in range(1, N_TP):
        remote(
            psend.at[t], prec.at[peer(u)], p_ss.at[t], p_rs.at[peer(u)], (i, peer(u))
        ).wait_recv()
    prec[t] = psend[t]
    relay_one(10, 14)
    def top_step(u, best):
        return jnp.maximum(best, prec[u, SESS])

    best = lax.fori_loop(1, N_TP, top_step, prec[0, SESS])

    def sum_step(u, carry):
        acc, tot = carry
        stat = prec[u, SESS]
        factor = jnp.exp(stat - best)
        new_acc = []
        new_tot = []
        for s in range(SESS):
            f = factor[:, 32 * s : 32 * s + 1]
            new_acc.append(acc[s] + f * prec[u, s])
            new_tot.append(tot[s] + f * stat[:, 32 * s + 16 : 32 * s + 17])
        return tuple(new_acc), tuple(new_tot)

    zero = jnp.zeros((16, HD), jnp.float32)
    none = jnp.zeros((16, 1), jnp.float32)
    acc, tot = lax.fori_loop(0, N_TP, sum_step, ((zero,) * SESS, (none,) * SESS))
    for s in range(SESS):
        osc[s] = acc[s] / tot[s]


    relay_one(14, 16)
    for r in (0, 1):
        row = osc[left[r]]
        for s in range(SESS):
            xsend[r, s] = jnp.where(arrives[r] == s, row, 0.0).astype(jnp.bfloat16)
    outs = [remote(xsend.at[r], xrecv.at[r], o_ss.at[r], o_rs.at[r], at(r + 1)) for r in (0, 1)]
    for copy in outs:
        copy.start()

    @pl.when(y == 2)
    def _():
        each(2, 4, lambda q: direct(2, q).start())

    places = []
    for step, lengths in enumerate((n1, n2)):
        for s in range(SESS):
            places.append((ints[8 * step + s, lengths[s] // PAGE] - low, lengths[s] % PAGE))
    for l in range(SLOTS):
        marks = []
        for step in range(2):
            sess, row = jnp.int32(0), jnp.int32(-1)
            for s in range(SESS):
                slot, at_row = places[step * SESS + s]
                sess = jnp.where(slot == l, s, sess)
                row = jnp.where(slot == l, at_row, row)
            marks.append((sess, one_hot(row)))
        (sess1, hot1), (sess2, hot2) = marks
        keep = 1 - hot1 - hot2

        def one(n, carry, l=l, sess1=sess1, sess2=sess2, hot1=hot1, hot2=hot2, keep=keep):
            token1 = spread(fr1[sess1, n // 8, pl.ds(n % 8, 1), :])
            token2 = spread(mine32[sess2, pl.ds(16 + n, 1), :])
            tile = cbuf[l, n].reshape(8, 16, HD) * keep + token1 * hot1 + token2 * hot2
            cbuf[l, n] = tile.reshape(PAGE, HD)
            return carry

        lax.fori_loop(0, 16, one, 0, unroll=4)

    @pl.when(last)
    def _():
        each(0, NCH, lambda k: first_leg(1, k).wait_send())

    @pl.when(y < 3)
    def _():
        each(0, NBIG, lambda q: direct(1, q).wait_send())

    for copy in outs:
        copy.wait_recv()
    for s in range(SESS):
        gone = jnp.where((left[0] == s) | (left[1] == s), 1, 0)
        came = xrecv[0, s].astype(jnp.float32) + xrecv[1, s].astype(jnp.float32)
        out_ref[s] = jnp.where(lower & (gone == 1), came, osc[s])

    for u in range(1, N_TP):
        meta_copy(u).wait_send()
        q_copy(u).wait_send()
        p_copy(peer(u)).wait_send()
    for copy in cross + outs:
        copy.wait_send()
    @pl.when(y == 0)
    def _():
        each(0, NCH, lambda k: second_leg(1, k).wait_send())

    @pl.when(odd)
    def _():
        each(0, HALF, lambda k: second_leg(2, k).wait_send())
        each(0, NBIG, lambda q: direct(2, q).wait_send())

    @pl.when(even)
    def _():
        each(0, HALF, lambda k: first_leg(2, k).wait_send())
        each(NBIG // 2, NBIG, lambda q: direct(2, q).wait_send())

    @pl.when(y == 0)
    def _():
        each(0, NCH, lambda k: second_leg(1, k).wait_recv())

    @pl.when(y > 0)
    def _():
        each(0, NBIG, lambda q: direct(1, q).wait_recv())

    @pl.when(odd)
    def _():
        each(0, NBIG, lambda q: direct(2, q).wait_recv())

    @pl.when(even)
    def _():
        each(0, HALF, lambda k: second_leg(2, k).wait_recv())
        each(NBIG // 2, NBIG, lambda q: direct(2, q).wait_recv())


def exchange(ints, moves, floats, cache):
    vmem = pl.BlockSpec(memory_space=pltpu.VMEM)
    smem = pl.BlockSpec(memory_space=pltpu.SMEM)
    hbm = pl.BlockSpec(memory_space=pl.ANY)
    dma = pltpu.SemaphoreType.DMA
    bf16, f32, i32 = jnp.bfloat16, jnp.float32, jnp.int32
    return pl.pallas_call(
        exchange_kernel,
        name="exchange",
        out_shape=(
            jax.ShapeDtypeStruct((SESS, 16, HD), f32),
            jax.ShapeDtypeStruct((2, TILES, PAGE, HD), bf16),
            jax.ShapeDtypeStruct((2, 8, 128), i32),
            jax.ShapeDtypeStruct((SLOTS, 16, PAGE, HD), bf16),
        ),
        in_specs=[smem, vmem, vmem, vmem, hbm],
        out_specs=(vmem, hbm, vmem, vmem),
        scratch_shapes=[
            pltpu.VMEM((2, TILES, PAGE, HD), bf16),
            pltpu.VMEM((TILES, PAGE, HD), bf16),
            pltpu.VMEM((2 * SESS, 16, PAGE, HD), bf16),
            pltpu.VMEM((8, 128), i32),
            pltpu.VMEM((N_TP, 8, 128), i32),
            pltpu.VMEM((2, 8, 128), i32),
            pltpu.VMEM((SESS, 32, HD), f32),
            pltpu.VMEM((SESS, 2, 8, HD), f32),
            pltpu.VMEM((SESS, 32, HD), bf16),
            pltpu.VMEM((2, SESS, 32, HD), bf16),
            pltpu.VMEM((SESS, 16, HD), f32),
            pltpu.VMEM((N_TP, SESS, 16, HD), bf16),
            pltpu.VMEM((N_TP, SESS + 1, 16, HD), f32),
            pltpu.VMEM((N_TP, SESS + 1, 16, HD), f32),
            pltpu.VMEM((SESS, 16, HD), f32),
            pltpu.VMEM((2, SESS, 16, HD), bf16),
            pltpu.VMEM((2, SESS, 16, HD), bf16),
            dma((SLOTS,)),
            dma((N_TP,)), dma((N_TP,)),
            dma((6,)), dma((6,)),
            dma((N_TP,)), dma((N_TP,)),
            dma((N_TP,)), dma((N_TP,)),
            dma((2,)), dma((2,)),
            dma((2, NCH + NBIG)), dma((2, NCH + NBIG)),
            dma((NCH,)), dma((NCH,)),
            dma((NCH,)),
        ],
        compiler_params=pltpu.CompilerParams(
            collective_id=1, has_side_effects=True, vmem_limit_bytes=44 * 1024 * 1024
        ),
    )(ints, moves, ints, floats, cache)


def assemble_kernel(came, ints, floats, rows, kept, recv, first_out, second_out, out, buf, sem):
    low = lax.axis_index("tp") * SLOTS
    targets = [came[r, 4 + 2 * r + c, 0] for r in range(2) for c in range(2)]
    for l in range(SLOTS):
        hit = functools.reduce(jnp.logical_or, [target == l for target in targets])

        @pl.when(jnp.logical_not(hit))
        def _():
            pltpu.make_async_copy(kept.at[l], out.at[l], sem.at[l]).start()
    tokens = [floats[s, 4:6].astype(jnp.float32) for s in range(SESS)]
    n2 = [ints[24, s] for s in range(SESS)]
    for e, target in enumerate(targets):
        row = jnp.int32(-1)
        token = tokens[0]
        for s in range(SESS):
            hit = (ints[8 + s, n2[s] // PAGE] - low == target) & (target >= 0)
            row = jnp.where(hit, n2[s] % PAGE, row)
            token = jnp.where(hit, tokens[s], token)
        hot = one_hot(row)
        keep = 1 - hot
        for n in range(16):
            new = spread(token[n // 8 : n // 8 + 1, (n % 8) * HD : (n % 8 + 1) * HD])
            tile = recv[e // 2, (e % 2) * 16 + n].reshape(8, 16, HD) * keep + new * hot
            buf[e, n] = tile.reshape(PAGE, HD)

        @pl.when(target >= 0)
        def _():
            pltpu.make_async_copy(buf.at[e], out.at[target], sem.at[target]).start()
    for h in range(KVH):
        first_out[:, h * HD : (h + 1) * HD] = rows[:, h, :].astype(first_out.dtype)
        second_out[:, h * HD : (h + 1) * HD] = rows[:, 8 + h, :].astype(second_out.dtype)
    for l in range(SLOTS):
        pltpu.make_async_copy(kept.at[l], out.at[l], sem.at[l]).wait()


def assemble(came, ints, floats, rows, kept, recv):
    vmem = pl.BlockSpec(memory_space=pltpu.VMEM)
    hbm = pl.BlockSpec(memory_space=pl.ANY)
    smem = pl.BlockSpec(memory_space=pltpu.SMEM)
    flat = jax.ShapeDtypeStruct((SESS, 8 * HD), jnp.bfloat16)
    return pl.pallas_call(
        assemble_kernel,
        name="assemble",
        out_shape=(flat, flat, jax.ShapeDtypeStruct(kept.shape, kept.dtype)),
        in_specs=[smem] * 2 + [vmem] * 2 + [hbm, vmem],
        out_specs=(vmem, vmem, hbm),
        scratch_shapes=[
            pltpu.VMEM((4, 16, PAGE, HD), jnp.bfloat16),
            pltpu.SemaphoreType.DMA((SLOTS,)),
        ],
        compiler_params=pltpu.CompilerParams(vmem_limit_bytes=16 * 1024 * 1024),
    )(came, ints, floats, rows, kept, recv)


def shards(
    cache_pool,
    first_query,
    second_query,
    first_fresh,
    second_fresh,
    first_tables,
    second_tables,
    first_lengths,
    second_lengths,
    page_moves,
):
    cache = cache_pool.reshape(SLOTS, 16, PAGE, HD)
    edge = ((0, 4), (0, 128 - first_tables.shape[1]))
    line = ((0, 7), (0, 128 - SESS))
    ints = jnp.concatenate(
        [
            jnp.pad(first_tables, edge, constant_values=-2),
            jnp.pad(second_tables, edge, constant_values=-2),
            jnp.pad(first_lengths[None], line),
            jnp.pad(second_lengths[None], line),
        ]
    )
    shape = (SESS, 6, first_query.shape[1])
    kind = lax.broadcasted_iota(jnp.int32, shape, 1)
    floats = jnp.where(
        kind < 4,
        jnp.pad(first_fresh, ((0, 0), (2, 2), (0, 0))),
        jnp.pad(second_fresh, ((0, 0), (4, 0), (0, 0))),
    )
    floats = jnp.where(kind == 0, lax.broadcast_in_dim(first_query, shape, (0, 2)), floats)
    floats = jnp.where(kind == 1, lax.broadcast_in_dim(second_query, shape, (0, 2)), floats)
    rows, recv, came, kept = exchange(ints, page_moves, floats, cache)
    first_out, second_out, cache_after = assemble(came, ints, floats, rows, kept, recv)
    return first_out, second_out, cache_after.reshape(cache_pool.shape)


def solution(mesh):
    placed = (
        P(("inst", "tp"), None, None, None, None),
        P("inst", "tp"),
        P("inst", "tp"),
        P("inst", None, None),
        P("inst", None, None),
        P("inst", None),
        P("inst", None),
        P("inst"),
        P("inst"),
        P(("inst", "tp"), None, None, None),
    )
    return jax.shard_map(
        shards,
        mesh=mesh,
        in_specs=placed,
        out_specs=(P("inst", "tp"), P("inst", "tp"), P(("inst", "tp"), None, None, None, None)),
        check_vma=False,
    )
```

```python
import functools

import jax
import jax.numpy as jnp
from jax import lax
from jax.experimental import pallas as pl
from jax.experimental.pallas import tpu as pltpu
from jax.sharding import PartitionSpec as P

HEADS = 128
KVH = 8
HD = 128
PAGE = 128
SLOTS = 12
SESS = 4
N_INST = 8
N_TP = 16
MESH = pl.DeviceIdType.MESH
TILES = 32
CHUNK = 2
NCH = TILES // CHUNK
HALF = NCH // 2
BIG = 8
NBIG = TILES // BIG


def iota(shape, dim):
    return lax.broadcasted_iota(jnp.int32, shape, dim)


def one_hot(row):
    hot = jnp.where(iota((PAGE, HD), 0) == row, 1.0, 0.0).astype(jnp.bfloat16)
    return hot.reshape(8, 16, HD)


def spread(row):
    return jnp.broadcast_to(row, (16, HD)).astype(jnp.bfloat16)[None]


def exchange_kernel(
    ints, moves, tabs, floats, cache,
    out_ref, recv_ref, rmeta_ref, cbuf,
    pay, rel, pages, meta, metas, xtab, mine32, fr1, mine, xmine, fr2, qall, psend, prec,
    osc, xsend, xrecv,
    load_sem, m_ss, m_rs, x_ss, x_rs, q_ss, q_rs, p_ss, p_rs, o_ss, o_rs,
    g_ss, g_rs, f_ss, f_rs, r_rs,
):
    i = lax.axis_index("inst")
    t = lax.axis_index("tp")
    xh = i // 4
    y = i % 4

    def inst(h, row):
        return lax.rem(h + 2, 2) * 4 + lax.rem(row + 4, 4)

    def at(k):
        return (lax.rem(i + k + N_INST, N_INST), t)

    def peer(u):
        return lax.rem(t + u, N_TP)

    def remote(src, dst, ss, rs, dev):
        return pltpu.make_async_remote_copy(src, dst, ss, rs, device_id=dev, device_id_type=MESH)

    loads = [pltpu.make_async_copy(cache.at[l], cbuf.at[l], load_sem.at[l]) for l in range(SLOTS)]
    for load in loads:
        load.start()

    barrier = pltpu.get_barrier_semaphore()
    for u in range(1, N_TP):
        pl.semaphore_signal(barrier, 1, device_id=(i, peer(u)), device_id_type=MESH)
    for k in range(1, N_INST):
        pl.semaphore_signal(barrier, 1, device_id=at(k), device_id_type=MESH)

    low = t * SLOTS
    n1 = [ints[16, s] for s in range(SESS)]
    n2 = [ints[24, s] for s in range(SESS)]
    slots, numbers = [], []
    for s in range(SESS):
        def look(p, found, s=s):
            slot0, slot1, page0, page1 = found
            v = ints[s, p] - low
            hit = (v >= 0) & (v < SLOTS)
            new = hit & (page0 < 0)
            return (
                jnp.where(new, v, slot0), jnp.where(hit, v, slot1),
                jnp.where(new, p, page0), jnp.where(hit, p, page1),
            )

        zero, none = jnp.int32(0), jnp.int32(-1)
        slot0, slot1, page0, page1 = lax.fori_loop(0, 32, look, (zero, zero, none, none), unroll=8)
        slots += [slot0, slot1]
        numbers += [page0, page1]

    rows8 = iota((8, 128), 0)
    sources, targets = {}, {}
    table = jnp.zeros((8, 128), jnp.int32)
    for r in (1, 2):
        b = lax.rem(i + r, N_INST)
        a_code = e_code = jnp.int32(-1)
        pairs = moves[0, b]
        for c in range(2):
            a, e = pairs[c, 0], pairs[c, 1]
            sources[r, c] = a
            a_code = jnp.maximum(a_code, jnp.where(a >= 0, low + a, -1))
            e_code = jnp.maximum(e_code, jnp.where(e >= 0, low + e, -1))
            table = jnp.where(rows8 == 4 + 2 * (r - 1) + c, e, table)
        table = jnp.where(rows8 == 2 * r - 2, a_code, table)
        table = jnp.where(rows8 == 2 * r - 1, e_code, table)
    meta[...] = table
    for s in range(SESS):
        flat = floats[s].astype(jnp.float32)
        for h in range(KVH):
            part = flat[:, h * HD : (h + 1) * HD]
            for row in range(2):
                mine32[s, 8 * row + h, :] = part[row]
                fr1[s, row, h, :] = part[2 + row]
                mine32[s, 16 + 8 * row + h, :] = part[4 + row]
    for s in range(SESS):
        mine[s] = mine32[s].astype(jnp.bfloat16)

    for load in loads:
        load.wait()

    def make_pay(r):
        for c in range(2):
            slot = jnp.maximum(sources[r, c], 0)
            sess = row = jnp.int32(0)
            for e in range(2 * SESS):
                mine_is = slots[e] == slot
                sess = jnp.where(mine_is, e // 2, sess)
                row = jnp.where(mine_is, n1[e // 2] - numbers[e] * PAGE, row)
            hot = one_hot(row)
            keep = 1 - hot

            def one(n, carry, slot=slot, sess=sess, hot=hot, keep=keep, c=c):
                fresh = spread(fr1[sess, n // 8, pl.ds(n % 8, 1), :])
                tile = cbuf[slot, n].reshape(8, 16, HD) * keep + fresh * hot
                pay[r - 1, c * 16 + n] = tile.reshape(PAGE, HD)
                return carry

            lax.fori_loop(0, 16, one, 0, unroll=4)

    make_pay(1)
    make_pay(2)
    pl.semaphore_wait(barrier, N_TP + N_INST - 2)

    def meta_copy(u):
        return remote(meta, metas.at[t], m_ss.at[u], m_rs.at[t], (i, peer(u)))

    for u in range(1, N_TP):
        meta_copy(u).start()
    cross = []
    for r in (1, 2):
        cross.append(remote(mine, xmine.at[r - 1], x_ss.at[r - 1], x_rs.at[r - 1], at(-r)))
        cross.append(remote(tabs.at[pl.ds(8, 8)], xtab.at[r - 1], x_ss.at[1 + r], x_rs.at[1 + r], at(-r)))
        cross.append(remote(meta, rmeta_ref.at[r - 1], x_ss.at[3 + r], x_rs.at[3 + r], at(r)))
    for copy in cross:
        copy.start()

    def chunk(k):
        return pl.ds(k * CHUNK, CHUNK)

    to_relay = {1: (inst(xh, y + 1), t), 2: (inst(xh, y - 1), t)}

    def direct(r, q):
        tiles = pl.ds(q * BIG, BIG)
        return remote(
            pay.at[r - 1, tiles], recv_ref.at[r - 1, tiles],
            g_ss.at[r - 1, NCH + q], g_rs.at[r - 1, NCH + q], at(r),
        )

    def first_leg(r, k):
        return remote(
            pay.at[r - 1, chunk(k)], rel.at[chunk(k)], g_ss.at[r - 1, k], r_rs.at[k], to_relay[r]
        )

    forward_to = {1: (inst(xh + 1, y), t), 2: (inst(xh + jnp.where(y == 1, 1, 0), y - 1), t)}

    def second_leg(r, k):
        return remote(
            rel.at[chunk(k)], recv_ref.at[r - 1, chunk(k)], f_ss.at[k], g_rs.at[r - 1, k], forward_to[r]
        )

    def each(low, high, fn):
        def body(k, carry):
            fn(k)
            return carry

        lax.fori_loop(low, high, body, 0)

    even = y % 2 == 0
    odd = y % 2 == 1
    last = y == 3
    @pl.when(even)
    def _():
        each(0, HALF, lambda k: first_leg(2, k).start())

    @pl.when(last)
    def _():
        each(0, NCH, lambda k: first_leg(1, k).start())

    @pl.when(y < 3)
    def _():
        each(0, NBIG, lambda q: direct(1, q).start())

    def relay_one(low, high):
        @pl.when(y == 0)
        def _():
            def step(k):
                first_leg(1, k).wait_recv()
                second_leg(1, k).start()

            each(low, high, step)

    def relay_two(low, high):
        @pl.when(odd)
        def _():
            def step(k):
                first_leg(2, k).wait_recv()
                second_leg(2, k).start()

            each(low, high, step)

    for u in range(1, N_TP):
        remote(meta, metas.at[peer(u)], m_ss.at[u], m_rs.at[peer(u)], (i, peer(u))).wait_recv()
    for copy in cross:
        copy.wait_recv()
    codes = meta[...]
    for u in range(1, N_TP):
        codes = jnp.maximum(codes, metas[peer(u)])
    left = []
    arrives = []
    for r in (1, 2):
        a_code = codes[2 * r - 2 : 2 * r - 1, :]
        e_code = codes[2 * r - 1 : 2 * r, :]
        left.append(jnp.minimum(jnp.max(jnp.where(tabs[0:8, :] == a_code, rows8, 0)), SESS - 1))
        arrives.append(jnp.minimum(jnp.max(jnp.where(xtab[r - 1] == e_code, rows8, 0)), SESS - 1))


    relay_two(0, 2)
    relay_one(0, 2)
    lower = iota((16, 128), 0) >= 8
    for s in range(SESS):
        own = mine[s].astype(jnp.float32)
        query = own[:16]
        fresh = own[16:]
        for r in (0, 1):
            other = xmine[r, arrives[r]].astype(jnp.float32)
            hit = jnp.where(left[r] == s, 1, 0)
            query = jnp.where(lower & (hit == 1), other[:16], query)
            fresh = jnp.where(hit == 1, other[16:], fresh)
        qall[t, s] = query.astype(jnp.bfloat16)
        fr2[s] = fresh

    def q_copy(u):
        return remote(qall.at[t], qall.at[t], q_ss.at[u], q_rs.at[t], (i, peer(u)))

    for u in range(1, N_TP):
        q_copy(u).start()


    @pl.when(odd)
    def _():
        each(0, 1, lambda q: direct(2, q).start())

    for s in range(SESS):
        for j in range(2):
            e = s * 2 + j
            slot = slots[e]
            row1 = n1[s] - numbers[e] * PAGE
            hot1 = one_hot(row1)
            hot2 = one_hot(row1 + 1)
            keep = 1 - hot1 - hot2

            def one(n, carry, slot=slot, hot1=hot1, hot2=hot2, keep=keep, s=s, e=e):
                fresh1 = spread(fr1[s, n // 8, pl.ds(n % 8, 1), :])
                fresh2 = spread(fr2[s, pl.ds(n, 1), :])
                tile = cbuf[slot, n].reshape(8, 16, HD) * keep + fresh1 * hot1 + fresh2 * hot2
                pages[e, n] = tile.reshape(PAGE, HD)
                return carry

            lax.fori_loop(0, 16, one, 0, unroll=4)

    relay_two(2, 4)
    relay_one(2, 4)
    for u in range(1, N_TP):
        remote(
            qall.at[t], qall.at[peer(u)], q_ss.at[u], q_rs.at[peer(u)], (i, peer(u))
        ).wait_recv()


    relay_two(4, 6)
    relay_one(4, 6)

    @pl.when(y == 0)
    def _():
        each(2, 4, lambda q: direct(2, q).start())

    lane = iota((32, 128), 1)
    step_two = (iota((32, 128), 0) // 8) % 2
    lane_group = lane // 16

    def p_copy(dst):
        return remote(psend.at[dst], prec.at[t], p_ss.at[dst], p_rs.at[t], (i, dst))

    def head_step(kk, carry):
        k = lax.rem(kk + t // 2 + 1, KVH)
        stat = jnp.zeros((32, 128), jnp.float32)
        for s in range(SESS):
            query = qall[pl.ds(2 * k, 2), s].reshape(32, HD)
            keys = pages[pl.ds(2 * s, 2), k].reshape(2 * PAGE, HD)
            both = lax.dot_general(
                query, keys, (((1,), (1,)), ((), ())), preferred_element_type=jnp.float32
            ) * (HD ** -0.5)
            tops, totals, sums = [], [], []
            for j in range(2):
                e = s * 2 + j
                scores = both[:, j * PAGE : (j + 1) * PAGE]
                visible = lane + numbers[e] * PAGE <= n1[s] + step_two
                top = jnp.max(jnp.where(visible, scores, -1e30), axis=1, keepdims=True)
                weight = jnp.where(visible, jnp.exp(scores - top), 0.0)
                tops.append(top)
                totals.append(jnp.sum(weight, axis=1, keepdims=True))
                sums.append(
                    jnp.dot(
                        weight.astype(jnp.bfloat16), pages[e, KVH + k],
                        preferred_element_type=jnp.float32,
                    )
                )
            top = jnp.maximum(tops[0], tops[1])
            f0 = jnp.exp(tops[0] - top)
            f1 = jnp.exp(tops[1] - top)
            psend[pl.ds(2 * k, 2), s] = (f0 * sums[0] + f1 * sums[1]).reshape(2, 16, HD)
            stat = jnp.where(lane_group == 2 * s, top, stat)
            stat = jnp.where(lane_group == 2 * s + 1, f0 * totals[0] + f1 * totals[1], stat)
        psend[pl.ds(2 * k, 2), SESS] = stat.reshape(2, 16, HD)
        for d in range(2):
            @pl.when(2 * k + d != t)
            def _():
                p_copy(2 * k + d).start()

        relay_two(6 + kk * 2 // 8, 6 + (kk + 1) * 2 // 8)

        @pl.when(odd & (kk == 7))
        def _():
            each(1, 4, lambda q: direct(2, q).start())

        return carry

    lax.fori_loop(0, KVH, head_step, 0)

    relay_one(6, 10)
    for u in range(1, N_TP):
        remote(
            psend.at[t], prec.at[peer(u)], p_ss.at[t], p_rs.at[peer(u)], (i, peer(u))
        ).wait_recv()
    prec[t] = psend[t]
    relay_one(10, 16)
    def top_step(u, best):
        return jnp.maximum(best, prec[u, SESS])

    best = lax.fori_loop(1, N_TP, top_step, prec[0, SESS])

    def sum_step(u, carry):
        acc, tot = carry
        stat = prec[u, SESS]
        factor = jnp.exp(stat - best)
        new_acc = []
        new_tot = []
        for s in range(SESS):
            f = factor[:, 32 * s : 32 * s + 1]
            new_acc.append(acc[s] + f * prec[u, s])
            new_tot.append(tot[s] + f * stat[:, 32 * s + 16 : 32 * s + 17])
        return tuple(new_acc), tuple(new_tot)

    zero = jnp.zeros((16, HD), jnp.float32)
    none = jnp.zeros((16, 1), jnp.float32)
    acc, tot = lax.fori_loop(0, N_TP, sum_step, ((zero,) * SESS, (none,) * SESS))
    for s in range(SESS):
        osc[s] = acc[s] / tot[s]


    for r in (0, 1):
        row = osc[left[r]]
        for s in range(SESS):
            xsend[r, s] = jnp.where(arrives[r] == s, row, 0.0).astype(jnp.bfloat16)
    outs = [remote(xsend.at[r], xrecv.at[r], o_ss.at[r], o_rs.at[r], at(r + 1)) for r in (0, 1)]
    for copy in outs:
        copy.start()

    @pl.when(y == 2)
    def _():
        each(2, 4, lambda q: direct(2, q).start())

    places = []
    for step, lengths in enumerate((n1, n2)):
        for s in range(SESS):
            places.append((ints[8 * step + s, lengths[s] // PAGE] - low, lengths[s] % PAGE))
    for l in range(SLOTS):
        marks = []
        for step in range(2):
            sess, row = jnp.int32(0), jnp.int32(-1)
            for s in range(SESS):
                slot, at_row = places[step * SESS + s]
                sess = jnp.where(slot == l, s, sess)
                row = jnp.where(slot == l, at_row, row)
            marks.append((sess, one_hot(row)))
        (sess1, hot1), (sess2, hot2) = marks
        keep = 1 - hot1 - hot2

        def one(n, carry, l=l, sess1=sess1, sess2=sess2, hot1=hot1, hot2=hot2, keep=keep):
            token1 = spread(fr1[sess1, n // 8, pl.ds(n % 8, 1), :])
            token2 = spread(mine32[sess2, pl.ds(16 + n, 1), :])
            tile = cbuf[l, n].reshape(8, 16, HD) * keep + token1 * hot1 + token2 * hot2
            cbuf[l, n] = tile.reshape(PAGE, HD)
            return carry

        lax.fori_loop(0, 16, one, 0, unroll=4)

    @pl.when(last)
    def _():
        each(0, NCH, lambda k: first_leg(1, k).wait_send())

    @pl.when(y < 3)
    def _():
        each(0, NBIG, lambda q: direct(1, q).wait_send())

    for copy in outs:
        copy.wait_recv()
    for s in range(SESS):
        gone = jnp.where((left[0] == s) | (left[1] == s), 1, 0)
        came = xrecv[0, s].astype(jnp.float32) + xrecv[1, s].astype(jnp.float32)
        out_ref[s] = jnp.where(lower & (gone == 1), came, osc[s])

    for u in range(1, N_TP):
        meta_copy(u).wait_send()
        q_copy(u).wait_send()
        p_copy(peer(u)).wait_send()
    for copy in cross + outs:
        copy.wait_send()
    @pl.when(y == 0)
    def _():
        each(0, NCH, lambda k: second_leg(1, k).wait_send())

    @pl.when(odd)
    def _():
        each(0, HALF, lambda k: second_leg(2, k).wait_send())
        each(0, NBIG, lambda q: direct(2, q).wait_send())

    @pl.when(even)
    def _():
        each(0, HALF, lambda k: first_leg(2, k).wait_send())
        each(NBIG // 2, NBIG, lambda q: direct(2, q).wait_send())

    @pl.when(y == 0)
    def _():
        each(0, NCH, lambda k: second_leg(1, k).wait_recv())

    @pl.when(y > 0)
    def _():
        each(0, NBIG, lambda q: direct(1, q).wait_recv())

    @pl.when(odd)
    def _():
        each(0, NBIG, lambda q: direct(2, q).wait_recv())

    @pl.when(even)
    def _():
        each(0, HALF, lambda k: second_leg(2, k).wait_recv())
        each(NBIG // 2, NBIG, lambda q: direct(2, q).wait_recv())


def exchange(ints, moves, floats, cache):
    vmem = pl.BlockSpec(memory_space=pltpu.VMEM)
    smem = pl.BlockSpec(memory_space=pltpu.SMEM)
    hbm = pl.BlockSpec(memory_space=pl.ANY)
    dma = pltpu.SemaphoreType.DMA
    bf16, f32, i32 = jnp.bfloat16, jnp.float32, jnp.int32
    return pl.pallas_call(
        exchange_kernel,
        name="exchange",
        out_shape=(
            jax.ShapeDtypeStruct((SESS, 16, HD), f32),
            jax.ShapeDtypeStruct((2, TILES, PAGE, HD), bf16),
            jax.ShapeDtypeStruct((2, 8, 128), i32),
            jax.ShapeDtypeStruct((SLOTS, 16, PAGE, HD), bf16),
        ),
        in_specs=[smem, vmem, vmem, vmem, hbm],
        out_specs=(vmem, hbm, vmem, vmem),
        scratch_shapes=[
            pltpu.VMEM((2, TILES, PAGE, HD), bf16),
            pltpu.VMEM((TILES, PAGE, HD), bf16),
            pltpu.VMEM((2 * SESS, 16, PAGE, HD), bf16),
            pltpu.VMEM((8, 128), i32),
            pltpu.VMEM((N_TP, 8, 128), i32),
            pltpu.VMEM((2, 8, 128), i32),
            pltpu.VMEM((SESS, 32, HD), f32),
            pltpu.VMEM((SESS, 2, 8, HD), f32),
            pltpu.VMEM((SESS, 32, HD), bf16),
            pltpu.VMEM((2, SESS, 32, HD), bf16),
            pltpu.VMEM((SESS, 16, HD), f32),
            pltpu.VMEM((N_TP, SESS, 16, HD), bf16),
            pltpu.VMEM((N_TP, SESS + 1, 16, HD), f32),
            pltpu.VMEM((N_TP, SESS + 1, 16, HD), f32),
            pltpu.VMEM((SESS, 16, HD), f32),
            pltpu.VMEM((2, SESS, 16, HD), bf16),
            pltpu.VMEM((2, SESS, 16, HD), bf16),
            dma((SLOTS,)),
            dma((N_TP,)), dma((N_TP,)),
            dma((6,)), dma((6,)),
            dma((N_TP,)), dma((N_TP,)),
            dma((N_TP,)), dma((N_TP,)),
            dma((2,)), dma((2,)),
            dma((2, NCH + NBIG)), dma((2, NCH + NBIG)),
            dma((NCH,)), dma((NCH,)),
            dma((NCH,)),
        ],
        compiler_params=pltpu.CompilerParams(
            collective_id=1, has_side_effects=True, vmem_limit_bytes=44 * 1024 * 1024
        ),
    )(ints, moves, ints, floats, cache)


def assemble_kernel(came, ints, floats, rows, kept, recv, first_out, second_out, out, buf, sem):
    low = lax.axis_index("tp") * SLOTS
    targets = [came[r, 4 + 2 * r + c, 0] for r in range(2) for c in range(2)]
    for l in range(SLOTS):
        hit = functools.reduce(jnp.logical_or, [target == l for target in targets])

        @pl.when(jnp.logical_not(hit))
        def _():
            pltpu.make_async_copy(kept.at[l], out.at[l], sem.at[l]).start()
    tokens = [floats[s, 4:6].astype(jnp.float32) for s in range(SESS)]
    n2 = [ints[24, s] for s in range(SESS)]
    for e, target in enumerate(targets):
        row = jnp.int32(-1)
        token = tokens[0]
        for s in range(SESS):
            hit = (ints[8 + s, n2[s] // PAGE] - low == target) & (target >= 0)
            row = jnp.where(hit, n2[s] % PAGE, row)
            token = jnp.where(hit, tokens[s], token)
        hot = one_hot(row)
        keep = 1 - hot
        for n in range(16):
            new = spread(token[n // 8 : n // 8 + 1, (n % 8) * HD : (n % 8 + 1) * HD])
            tile = recv[e // 2, (e % 2) * 16 + n].reshape(8, 16, HD) * keep + new * hot
            buf[e, n] = tile.reshape(PAGE, HD)

        @pl.when(target >= 0)
        def _():
            pltpu.make_async_copy(buf.at[e], out.at[target], sem.at[target]).start()
    for h in range(KVH):
        first_out[:, h * HD : (h + 1) * HD] = rows[:, h, :].astype(first_out.dtype)
        second_out[:, h * HD : (h + 1) * HD] = rows[:, 8 + h, :].astype(second_out.dtype)
    for l in range(SLOTS):
        pltpu.make_async_copy(kept.at[l], out.at[l], sem.at[l]).wait()


def assemble(came, ints, floats, rows, kept, recv):
    vmem = pl.BlockSpec(memory_space=pltpu.VMEM)
    hbm = pl.BlockSpec(memory_space=pl.ANY)
    smem = pl.BlockSpec(memory_space=pltpu.SMEM)
    flat = jax.ShapeDtypeStruct((SESS, 8 * HD), jnp.bfloat16)
    return pl.pallas_call(
        assemble_kernel,
        name="assemble",
        out_shape=(flat, flat, jax.ShapeDtypeStruct(kept.shape, kept.dtype)),
        in_specs=[smem] * 2 + [vmem] * 2 + [hbm, vmem],
        out_specs=(vmem, vmem, hbm),
        scratch_shapes=[
            pltpu.VMEM((4, 16, PAGE, HD), jnp.bfloat16),
            pltpu.SemaphoreType.DMA((SLOTS,)),
        ],
        compiler_params=pltpu.CompilerParams(vmem_limit_bytes=16 * 1024 * 1024),
    )(came, ints, floats, rows, kept, recv)


def shards(
    cache_pool,
    first_query,
    second_query,
    first_fresh,
    second_fresh,
    first_tables,
    second_tables,
    first_lengths,
    second_lengths,
    page_moves,
):
    cache = cache_pool.reshape(SLOTS, 16, PAGE, HD)
    edge = ((0, 4), (0, 128 - first_tables.shape[1]))
    line = ((0, 7), (0, 128 - SESS))
    ints = jnp.concatenate(
        [
            jnp.pad(first_tables, edge, constant_values=-2),
            jnp.pad(second_tables, edge, constant_values=-2),
            jnp.pad(first_lengths[None], line),
            jnp.pad(second_lengths[None], line),
        ]
    )
    shape = (SESS, 6, first_query.shape[1])
    kind = lax.broadcasted_iota(jnp.int32, shape, 1)
    floats = jnp.where(
        kind < 4,
        jnp.pad(first_fresh, ((0, 0), (2, 2), (0, 0))),
        jnp.pad(second_fresh, ((0, 0), (4, 0), (0, 0))),
    )
    floats = jnp.where(kind == 0, lax.broadcast_in_dim(first_query, shape, (0, 2)), floats)
    floats = jnp.where(kind == 1, lax.broadcast_in_dim(second_query, shape, (0, 2)), floats)
    rows, recv, came, kept = exchange(ints, page_moves, floats, cache)
    first_out, second_out, cache_after = assemble(came, ints, floats, rows, kept, recv)
    return first_out, second_out, cache_after.reshape(cache_pool.shape)


def solution(mesh):
    placed = (
        P(("inst", "tp"), None, None, None, None),
        P("inst", "tp"),
        P("inst", "tp"),
        P("inst", None, None),
        P("inst", None, None),
        P("inst", None),
        P("inst", None),
        P("inst"),
        P("inst"),
        P(("inst", "tp"), None, None, None),
    )
    return jax.shard_map(
        shards,
        mesh=mesh,
        in_specs=placed,
        out_specs=(P("inst", "tp"), P("inst", "tp"), P(("inst", "tp"), None, None, None, None)),
        check_vma=False,
    )
```
